32 devices in a mesh: rep: 2 (over x), kv: 4 (over y, core), tp: 4 (over z).
Axes of the slice: x: 2, y: 2, z: 4, core: 2. Of those that a mesh axis runs over, the one named last changes fastest.
Arguments:
- token_state: bfloat16 [32, 1280], P('kv'), may hold values from -6 to 6
- attn_gain: float32 [1280], replicated, may hold values from 0.1 to 1.9
- qkv_weight: bfloat16 [1280, 3840], P(None, 'tp'), may hold values from -0.15625 to 0.15625
- out_weight: bfloat16 [1280, 1280], P('tp'), may hold values from -0.15625 to 0.15625
- mlp_gain: float32 [1280], replicated, may hold values from 0.1 to 1.9
- up_weight: bfloat16 [1280, 1280], P(None, 'tp'), may hold values from -0.15625 to 0.15625
- down_weight: bfloat16 [1280, 1280], P('tp'), may hold values from -0.15625 to 0.15625
- kv_cache: bfloat16 [2, 44, 512, 2560], P('rep', 'kv', None, 'tp'), as said below
- home_replica: int32 [32], replicated, may hold values from 0 to 1, as said below
- moving: int32 [32], replicated, may hold values 0 or 1
- cache_length: int32 [32], replicated, may hold values from 1 to 5632, as said below
- block_owner: int32 [2, 44], P('rep', 'kv'), may hold values from 0 to 32, as said below
- block_index: int32 [2, 44], P('rep', 'kv'), may hold values from 0 to 10, as said below
Outputs:
- hidden_out: float32 [2, 32, 1280], P('rep', 'kv')
- new_entries: float32 [2, 32, 2560], P('rep', 'kv', 'tp')
The draws below stay inside these ranges and needn't reach their ends.
Inputs may be any that keep to these rules, and one draw needn't show every extreme that they name: `home_replica`: both replicas hold at least one slot. `cache_length`: a slot's cache lies whole in the pool of its home replica; one slot of each replica has exactly 5632 tokens. `block_owner`: a slot owns exactly ceil(cache_length / 512) blocks, all in the pool of its home replica; 32 marks a free block. `block_index`: the blocks of one slot carry 0 to ceil(cache_length / 512) - 1, each once; free blocks carry 0. `kv_cache`: keys may be large in a few tokens.
All inputs are finite; a program needn't handle non-finite values.
Results may differ from the reference program's by a relative error of at most 0.0061.
Values may be sent and summed in bfloat16 or wider, within the bound.
A program may use at most 128 MiB of HBM per device.

```python
import jax
import jax.numpy as jnp
from jax import lax

D = 1280
HEADS = 16
HD = 80
FF = 1280
BLOCK = 512
RQ = 32
NBLK = 44
MAXB = 11
N_REP = 2


def layout(key):
    layout_key = jax.random.fold_in(key, 7001)
    streams = jax.random.split(layout_key, 8)
    slots = jnp.arange(RQ, dtype=jnp.int32)
    home_pick = jax.random.randint(streams[0], (RQ,), 0, 3)
    home_slot = (home_pick >= 2).astype(jnp.int32)
    long_zero = jax.random.randint(streams[1], (), 0, RQ)
    long_one = (long_zero + 1 + jax.random.randint(streams[2], (), 0, RQ - 1)) % RQ
    home_slot = jnp.where(slots == long_zero, 0, home_slot)
    home_slot = jnp.where(slots == long_one, 1, home_slot).astype(jnp.int32)
    shift_draw = jax.random.randint(streams[3], (RQ,), 0, 24)
    spare_want = jnp.right_shift(jnp.full((RQ,), MAXB - 1, jnp.int32), shift_draw)
    extras = jnp.zeros((RQ,), jnp.int32)
    longest = [long_zero, long_one]
    for replica in range(2):
        homed_here = home_slot == replica
        headroom = NBLK - jnp.sum(homed_here.astype(jnp.int32)) - (MAXB - 1)
        wanted = jnp.where(homed_here & (slots != longest[replica]), spare_want, 0)
        before = jnp.cumsum(wanted) - wanted
        granted = jnp.clip(headroom - before, 0, wanted)
        extras = extras + granted + jnp.where(slots == longest[replica], MAXB - 1, 0)
    counts = 1 + extras
    tail_tokens = jax.random.randint(streams[4], (RQ,), 1, BLOCK + 1)
    lengths = (counts - 1) * BLOCK + tail_tokens
    lengths = jnp.where((slots == long_zero) | (slots == long_one), MAXB * BLOCK, lengths).astype(jnp.int32)
    owner_rows = []
    index_rows = []
    sequence_pos = jnp.arange(NBLK, dtype=jnp.int32)
    for replica in range(2):
        sizes_here = jnp.where(home_slot == replica, counts, 0)
        run_ends = jnp.cumsum(sizes_here)
        run_starts = run_ends - sizes_here
        owner_seq = jnp.sum((run_ends[None, :] <= sequence_pos[:, None]).astype(jnp.int32), axis=1)
        index_seq = jnp.where(owner_seq < RQ, sequence_pos - run_starts[jnp.minimum(owner_seq, RQ - 1)], 0)
        source_pos = jax.random.permutation(streams[5 + replica], sequence_pos).astype(jnp.int32)
        owner_rows.append(owner_seq[source_pos])
        index_rows.append(index_seq[source_pos])
    return (home_slot, lengths, jnp.stack(owner_rows).astype(jnp.int32), jnp.stack(index_rows).astype(jnp.int32))


def draw_home_replica(key, part):
    return layout(key)[0]


def draw_cache_length(key, part):
    return layout(key)[1]


def draw_block_owner(key, part):
    return layout(key)[2]


def draw_block_index(key, part):
    return layout(key)[3]


def draw_kv_cache(key, part):
    total_blocks = N_REP * NBLK

    def one_block(block_number):
        block_key = jax.random.fold_in(key, block_number)
        streams = jax.random.split(block_key, 1)
        drawn_draw = jax.random.normal(streams[0], (BLOCK, HEADS, 2, HD), jnp.float32)
        drawn_draw = drawn_draw * jnp.array([2.0, 1.0], jnp.float32)[None, None, :, None]
        return drawn_draw.reshape(BLOCK, HEADS * 2 * HD).astype(jnp.bfloat16)
    drawn = lax.map(one_block, jnp.arange(total_blocks, dtype=jnp.int32))
    return drawn.reshape(N_REP, NBLK, BLOCK, HEADS * 2 * HD)


def plant(values, rng, least, top_value):
    longest = values.shape.index(max(values.shape))
    spots = []
    for shift in (0, 1):
        where = [jax.random.randint(jax.random.fold_in(rng, axis), (), 0, length) for axis, length in enumerate(values.shape)]
        where[longest] = (where[longest] + shift) % values.shape[longest]
        spots.append(tuple(where))
    return values.at[spots[0]].set(least).at[spots[1]].set(top_value)


def shard_levels(own_key, extent, shards, least, high):
    def one(position, parts):
        heights = jax.random.uniform(jax.random.fold_in(jax.random.fold_in(own_key, 6), position), (parts,), jnp.float32, least / len(shards), high / len(shards))
        return jnp.repeat(jnp.exp(heights), extent[position] // parts).reshape((-1,) + (1,) * (len(extent) - position - 1))

    gain = one(*shards[0])
    for cut in shards[1:]:
        gain = gain * one(*cut)
    return gain


def scatter_about(own_key, extent, width, most, cuts=(), kind=jnp.bfloat16):
    values = width * jax.random.normal(own_key, extent, jnp.float32)
    if cuts:
        values = values * shard_levels(own_key, extent, cuts, -0.22, 0.18)
    return jnp.clip(values, -most, most).astype(kind)


def setup_inputs(seed: int = 0) -> dict:
    keys = jax.random.split(jax.random.key(seed), 14)
    return {
        "token_state": scatter_about(keys[0], (RQ, D), 1.0, 6.0, ((0, 4),)),
        "attn_gain": jnp.clip(1.0 + 0.18 * jax.random.normal(keys[1], (D,), jnp.float32), 0.1, 1.9),
        "qkv_weight": scatter_about(keys[2], (D, HEADS * 3 * HD), D ** -0.5, 0.15625, ((1, 4),)),
        "out_weight": scatter_about(keys[3], (HEADS * HD, D), (HEADS * HD) ** -0.5, 0.15625, ((0, 4),)),
        "mlp_gain": jnp.clip(1.0 + 0.18 * jax.random.normal(keys[4], (D,), jnp.float32), 0.1, 1.9),
        "up_weight": scatter_about(keys[5], (D, FF), D ** -0.5, 0.15625, ((1, 4),)),
        "down_weight": scatter_about(keys[6], (FF, D), FF ** -0.5, 0.15625, ((0, 4),)),
        "kv_cache": draw_kv_cache(jax.random.fold_in(keys[13], 71), 0),
        "home_replica": draw_home_replica(jax.random.fold_in(keys[13], 71), 0),
        "moving": plant((jax.random.randint(keys[9], (RQ,), 0, 4) < 1).astype(jnp.int32), jax.random.fold_in(keys[9], 1), 0, 1),
        "cache_length": draw_cache_length(jax.random.fold_in(keys[13], 71), 0),
        "block_owner": draw_block_owner(jax.random.fold_in(keys[13], 71), 0),
        "block_index": draw_block_index(jax.random.fold_in(keys[13], 71), 0),
    }


very_low = -1e+30
norm_eps = 1e-06

def root_norm(values_in, gain_vector):
    values_in = values_in.astype(jnp.float32)
    scaled = values_in * lax.rsqrt(lax.optimization_barrier(jnp.mean(values_in * values_in, axis=-1, keepdims=True)) + norm_eps)
    return scaled * gain_vector

def reference(token_state, attn_gain, qkv_weight, out_weight, mlp_gain, up_weight, down_weight, kv_cache, home_replica, moving, cache_length, block_owner, block_index):
    requests = token_state.shape[0]
    normed = root_norm(token_state, attn_gain).astype(jnp.bfloat16)
    projected = jnp.dot(normed, qkv_weight, preferred_element_type=jnp.float32).reshape(requests, HEADS, 3, HD)
    query = (projected[:, :, 0] * HD ** (-0.5)).astype(jnp.bfloat16)
    fresh_pairs = projected[:, :, 1:].astype(jnp.bfloat16)
    block_count = N_REP * NBLK
    blocks = kv_cache.reshape(block_count, BLOCK, HEADS, 2, HD)
    owners = block_owner.reshape(block_count)
    block_starts = block_index.reshape(block_count)
    is_owned = owners < requests
    clipped = jnp.minimum(owners, requests - 1).astype(jnp.int32)
    offsets = jnp.arange(BLOCK, dtype=jnp.int32)

    def score_block(packed):
        cache_block, owner_slot, block_start, owned_here = packed
        raw_scores = jnp.einsum('hd,thd->th', query[owner_slot].astype(jnp.float32), cache_block[:, :, 0].astype(jnp.float32), precision=lax.Precision.HIGHEST)
        usable = owned_here & (block_start * BLOCK + offsets < cache_length[owner_slot])
        return (jnp.where(usable[:, None], raw_scores, very_low), usable)
    scores, usable = lax.map(score_block, (blocks, clipped, block_starts, is_owned))
    self_score = lax.optimization_barrier(jnp.sum(query.astype(jnp.float32) * fresh_pairs[:, :, 0].astype(jnp.float32), axis=-1))
    block_peak = lax.optimization_barrier(jnp.max(scores, axis=1))
    onehot = (clipped[:, None] == jnp.arange(requests, dtype=jnp.int32)[None, :]) & is_owned[:, None]
    cache_peak = lax.optimization_barrier(jnp.max(jnp.where(onehot[:, :, None], block_peak[:, None, :], very_low), axis=0))
    top_score = jnp.maximum(cache_peak, self_score)

    def weigh_block(packed):
        cache_block, block_scores, block_usable, owner_slot = packed
        weights = jnp.where(block_usable[:, None], jnp.exp(block_scores - top_score[owner_slot][None, :]), 0.0)
        block_total = lax.optimization_barrier(jnp.sum(weights, axis=0))
        rounded = lax.optimization_barrier(weights.astype(jnp.bfloat16))
        block_acc = jnp.einsum('th,thd->hd', rounded.astype(jnp.float32), cache_block[:, :, 1].astype(jnp.float32), precision=lax.Precision.HIGHEST)
        return (block_total, block_acc)
    totals, accums = lax.map(weigh_block, (blocks, scores, usable, clipped))
    selector = onehot.astype(jnp.float32)
    cache_total = jnp.einsum('bq,bh->qh', selector, totals, precision=lax.Precision.HIGHEST)
    cache_acc = jnp.einsum('bq,bhd->qhd', selector, accums, precision=lax.Precision.HIGHEST)
    self_weight = jnp.exp(self_score - top_score)
    rounded_self = lax.optimization_barrier(self_weight.astype(jnp.bfloat16)).astype(jnp.float32)
    denominator = cache_total + self_weight
    numerator = cache_acc + rounded_self[..., None] * fresh_pairs[:, :, 1].astype(jnp.float32)
    attended = (numerator / denominator[..., None]).astype(jnp.bfloat16).reshape(requests, HEADS * HD)
    residual = token_state.astype(jnp.float32) + jnp.dot(attended, out_weight, preferred_element_type=jnp.float32)
    normed_mlp = root_norm(residual, mlp_gain).astype(jnp.bfloat16)
    activated = jax.nn.gelu(jnp.dot(normed_mlp, up_weight, preferred_element_type=jnp.float32), approximate=True).astype(jnp.bfloat16)
    result = residual + jnp.dot(activated, down_weight, preferred_element_type=jnp.float32)
    target = jnp.bitwise_xor(home_replica, moving)
    replicas = jnp.arange(N_REP, dtype=jnp.int32)
    served = target[None, :] == replicas[:, None]
    hidden_out = jnp.where(served[:, :, None], result[None], jnp.zeros_like(result)[None])
    entries = projected[:, :, 1:].reshape(requests, HEADS * 2 * HD)
    new_entries = jnp.where(served[:, :, None], entries[None], jnp.zeros_like(entries)[None])
    return (hidden_out, new_entries)
```

```python
import functools

import jax
import jax.numpy as jnp
from jax import lax
from jax.experimental import pallas as pl
from jax.experimental.pallas import tpu as pltpu
from jax.sharding import PartitionSpec as P

HD = 80
PAIR = 2 * HD

very_low = -1e30
norm_eps = 1e-06

MESH = pl.DeviceIdType.MESH
BF16 = jnp.bfloat16
F32 = jnp.float32


def root_norm(values_in, gain_vector):
    values_in = values_in.astype(F32)
    scaled = values_in * lax.rsqrt(
        jnp.mean(values_in * values_in, axis=-1, keepdims=True) + norm_eps
    )
    return scaled * gain_vector


def gelu_tanh(x):
    return 0.5 * x * (1.0 + jnp.tanh(0.7978845608028654 * (x + 0.044715 * (x * x * x))))


def dot_last(left, right):
    return lax.dot_general(left, right, (((1,), (1,)), ((), ())), preferred_element_type=F32)


def dot_plain(left, right):
    return lax.dot_general(left, right, (((1,), (0,)), ((), ())), preferred_element_type=F32)


def kernel(
    sizes,
    state_ref,
    attn_gain_ref,
    mlp_gain_ref,
    home_ref,
    moving_ref,
    length_ref,
    owner_ref,
    index_ref,
    qkv_hbm,
    out_hbm,
    up_hbm,
    down_hbm,
    cache_hbm,
    hidden_ref,
    entries_ref,
    w_query,
    w_pair,
    w_out,
    w_up,
    w_down,
    cache,
    q_all,
    q_rows,
    stat_send,
    sums_send,
    stat_recv,
    sums_recv,
    part_out,
    part_down,
    load_sem,
    cache_sem,
    q_send_sem,
    q_recv_sem,
    stat_send_sem,
    stat_recv_sem,
    sums_send_sem,
    sums_recv_sem,
    out_send_sem,
    out_recv_sem,
    down_send_sem,
    down_recv_sem,
):
    reps, kvs, tps, heads, blocks, tokens, rows, requests = sizes
    width = heads * PAIR
    sources = reps * kvs
    rep = lax.axis_index("rep")
    kv = lax.axis_index("kv")
    tp = lax.axis_index("tp")
    me = rep * kvs + kv

    def source_id(number):
        return {"rep": lax.div(number, kvs), "kv": lax.rem(number, kvs)}

    barrier = pltpu.get_barrier_semaphore()
    for step in range(1, sources):
        pl.semaphore_signal(
            barrier,
            inc=1,
            device_id=source_id(lax.rem(me + step, sources)),
            device_id_type=MESH,
        )
    for step in range(1, tps):
        pl.semaphore_signal(
            barrier, inc=1, device_id={"tp": lax.rem(tp + step, tps)}, device_id_type=MESH
        )

    query_loads, pair_loads, out_loads = [], [], []
    for h in range(heads):
        query_loads.append(
            pltpu.make_async_copy(
                qkv_hbm.at[pl.ds(h * 3 * HD, PAIR)],
                w_query.at[pl.ds(h * PAIR, PAIR)],
                load_sem.at[h],
            )
        )
        pair_loads.append(
            pltpu.make_async_copy(
                qkv_hbm.at[pl.ds(h * 3 * HD + HD, PAIR)],
                w_pair.at[pl.ds(h * PAIR, PAIR)],
                load_sem.at[heads + h],
            )
        )
        for half in range(2):
            out_loads.append(
                pltpu.make_async_copy(
                    out_hbm.at[pl.ds(h * HD, HD)],
                    w_out.at[pl.ds(h * PAIR + half * HD, HD)],
                    load_sem.at[2 * heads + 2 * h + half],
                )
            )
    up_load = pltpu.make_async_copy(up_hbm, w_up, load_sem.at[4 * heads])
    down_load = pltpu.make_async_copy(down_hbm, w_down, load_sem.at[4 * heads + 1])
    cache_loads = [
        pltpu.make_async_copy(cache_hbm.at[0, b], cache.at[b], cache_sem.at[b])
        for b in range(blocks)
    ]
    for copy in query_loads + cache_loads + pair_loads + out_loads + [up_load, down_load]:
        copy.start()

    state = state_ref[...].astype(F32)
    normed = root_norm(state, attn_gain_ref[...]).astype(BF16)
    for copy in query_loads:
        copy.wait()
    query = (dot_last(normed, w_query[...]) * HD ** (-0.5)).astype(BF16)
    q_all[kv] = query

    pl.semaphore_wait(barrier, sources - 1 + tps - 1)

    q_sends = []
    for step in range(1, kvs):
        copy = pltpu.make_async_remote_copy(
            src_ref=q_all.at[kv],
            dst_ref=q_all.at[kv],
            send_sem=q_send_sem.at[step],
            recv_sem=q_recv_sem.at[kv],
            device_id={"kv": lax.rem(kv + step, kvs)},
            device_id_type=MESH,
        )
        copy.start()
        q_sends.append(copy)

    for copy in pair_loads:
        copy.wait()
    pairs = dot_last(normed, w_pair[...])
    fresh = pairs.astype(BF16).astype(F32)
    lane = lax.broadcasted_iota(jnp.int32, (1, width), 1)
    lane_head = sum((lane >= h * PAIR).astype(jnp.int32) for h in range(1, heads))
    is_value = (lane - lane_head * PAIR) >= HD
    small_lane = lax.broadcasted_iota(jnp.int32, (1, 128), 1)
    self_products = jnp.where(is_value, 0.0, query.astype(F32) * fresh)
    self_score = jnp.full((rows, 128), very_low, F32)
    for h in range(heads):
        score = jnp.sum(jnp.where(lane_head == h, self_products, 0.0), axis=1, keepdims=True)
        self_score = jnp.where(small_lane == h, score, self_score)
    fresh_values = jnp.where(is_value, fresh, 0.0)

    row_number = lax.broadcasted_iota(jnp.int32, (rows, 1), 0)
    target = jnp.zeros((rows, 1), jnp.int32)
    for i in range(rows):
        slot = kv * rows + i
        aim = jnp.bitwise_xor(home_ref[slot], moving_ref[slot])
        target = jnp.where(row_number == i, aim, target)
    served_here = target == rep
    entries_ref[0] = jnp.where(served_here, pairs, 0.0)

    for step in range(1, kvs):
        other = lax.rem(kv + step, kvs)
        pltpu.make_async_remote_copy(
            src_ref=q_all.at[other],
            dst_ref=q_all.at[other],
            send_sem=q_send_sem.at[step],
            recv_sem=q_recv_sem.at[other],
            device_id={"kv": other},
            device_id_type=MESH,
        ).wait_recv()
    q_rows[...] = q_all[...].astype(F32).reshape(requests, width)

    head_row = lax.broadcasted_iota(jnp.int32, (8, 1), 0)
    key_mask = (lane_head == head_row) & ~is_value
    value_mask = (lane_head == head_row) & is_value
    token_lane = lax.broadcasted_iota(jnp.int32, (1, tokens), 1)

    owners, limits, scores, peaks = [], [], [], []
    for b in range(blocks):
        owner = owner_ref[0, b]
        clipped = jnp.minimum(owner, requests - 1)
        limit = jnp.where(
            owner < requests, length_ref[clipped] - index_ref[0, b] * tokens, 0
        )
        q_row = q_rows[pl.ds(clipped, 1), :]
        block_query = jnp.where(key_mask, q_row, 0.0).astype(BF16)
        cache_loads[b].wait()
        score = dot_last(block_query, cache[b])
        score = jnp.where(token_lane < limit, score, very_low)
        owners.append(owner)
        limits.append(limit)
        scores.append(score)
        peaks.append(jnp.max(score, axis=1, keepdims=True))

    slot_row = lax.broadcasted_iota(jnp.int32, (requests, 1), 0)
    sums = jnp.zeros((requests, width), F32)
    stats = jnp.where(small_lane < 8, very_low, 0.0) + jnp.zeros((requests, 128), F32)
    for b in range(blocks):
        shift = peaks[b]
        for other in range(blocks):
            if other != b:
                shift = jnp.where(
                    owners[other] == owners[b], jnp.maximum(shift, peaks[other]), shift
                )
        weight = jnp.where(token_lane < limits[b], jnp.exp(scores[b] - shift), 0.0)
        total = jnp.sum(weight, axis=1, keepdims=True)
        acc = dot_plain(weight.astype(BF16), cache[b])
        acc_row = jnp.sum(jnp.where(value_mask, acc, 0.0), axis=0, keepdims=True)
        stat_row = jnp.sum(
            jnp.where(
                small_lane == head_row, shift, jnp.where(small_lane == head_row + 8, total, 0.0)
            ),
            axis=0,
            keepdims=True,
        )
        mine = slot_row == owners[b]
        sums = sums + jnp.where(mine, acc_row, 0.0)
        stats = jnp.where(
            mine, jnp.where(small_lane < 8, stat_row, stats + stat_row), stats
        )
    stat_send[...] = stats.reshape(kvs, rows, 128)
    sums_send[...] = sums.reshape(kvs, rows, width).astype(BF16)

    partial_sends = []
    for step in range(1, sources):
        to = lax.rem(me + step, sources)
        to_kv = lax.rem(to, kvs)
        for src, dst, send_sem, recv_sem in (
            (stat_send, stat_recv, stat_send_sem, stat_recv_sem),
            (sums_send, sums_recv, sums_send_sem, sums_recv_sem),
        ):
            copy = pltpu.make_async_remote_copy(
                src_ref=src.at[to_kv],
                dst_ref=dst.at[me],
                send_sem=send_sem.at[step],
                recv_sem=recv_sem.at[me],
                device_id=source_id(to),
                device_id_type=MESH,
            )
            copy.start()
            partial_sends.append(copy)
    stat_recv[me] = stat_send[kv]
    sums_recv[me] = sums_send[kv]
    for step in range(1, sources):
        other = lax.rem(me + step, sources)
        for dst, send_sem, recv_sem in (
            (stat_recv, stat_send_sem, stat_recv_sem),
            (sums_recv, sums_send_sem, sums_recv_sem),
        ):
            pltpu.make_async_remote_copy(
                src_ref=dst.at[other],
                dst_ref=dst.at[other],
                send_sem=send_sem.at[step],
                recv_sem=recv_sem.at[other],
                device_id=source_id(other),
                device_id_type=MESH,
            ).wait_recv()

    def over_lanes(values):
        wide = jnp.broadcast_to(values[:, heads - 1 : heads], (rows, width))
        for h in reversed(range(heads - 1)):
            wide = jnp.where(lane < (h + 1) * PAIR, values[:, h : h + 1], wide)
        return wide

    top = self_score
    for s in range(sources):
        top = jnp.maximum(top, stat_recv[s])
    in_heads = small_lane < heads
    self_weight = jnp.exp(self_score - top)
    denominator = self_weight
    factors = []
    for s in range(sources):
        stat = stat_recv[s]
        factor = jnp.exp(stat - top)
        factors.append(factor)
        denominator = denominator + pltpu.roll(stat, 120, 1) * factor
    denominator = jnp.where(in_heads, denominator, 1.0)
    numerator = over_lanes(self_weight.astype(BF16).astype(F32)) * fresh_values
    for s in range(sources):
        numerator = numerator + over_lanes(factors[s]) * sums_recv[s].astype(F32)
    attended = (numerator / over_lanes(denominator)).astype(BF16)

    def summed_over_tp(part, buffer, send_sem, recv_sem):
        buffer[tp] = part.astype(BF16)
        sends = []
        for step in range(1, tps):
            copy = pltpu.make_async_remote_copy(
                src_ref=buffer.at[tp],
                dst_ref=buffer.at[tp],
                send_sem=send_sem.at[step],
                recv_sem=recv_sem.at[tp],
                device_id={"tp": lax.rem(tp + step, tps)},
                device_id_type=MESH,
            )
            copy.start()
            sends.append(copy)
        for step in range(1, tps):
            other = lax.rem(tp + step, tps)
            pltpu.make_async_remote_copy(
                src_ref=buffer.at[other],
                dst_ref=buffer.at[other],
                send_sem=send_sem.at[step],
                recv_sem=recv_sem.at[other],
                device_id={"tp": other},
                device_id_type=MESH,
            ).wait_recv()
        total = buffer[0].astype(F32)
        for t in range(1, tps):
            total = total + buffer[t].astype(F32)
        return total, sends

    for copy in out_loads:
        copy.wait()
    attn_out, out_sends = summed_over_tp(
        dot_plain(attended, w_out[...]), part_out, out_send_sem, out_recv_sem
    )
    residual = state + attn_out
    normed_mlp = root_norm(residual, mlp_gain_ref[...]).astype(BF16)
    up_load.wait()
    activated = gelu_tanh(dot_last(normed_mlp, w_up[...])).astype(BF16)
    down_load.wait()
    mlp_out, down_sends = summed_over_tp(
        dot_plain(activated, w_down[...]), part_down, down_send_sem, down_recv_sem
    )
    hidden_ref[0] = jnp.where(served_here, residual + mlp_out, 0.0)
    for copy in q_sends + partial_sends + out_sends + down_sends:
        copy.wait_send()


def body(
    reps,
    kvs,
    tps,
    token_state,
    attn_gain,
    qkv_weight,
    out_weight,
    mlp_gain,
    up_weight,
    down_weight,
    kv_cache,
    home_replica,
    moving,
    cache_length,
    block_owner,
    block_index,
):
    rows, model = token_state.shape
    requests = home_replica.shape[0]
    heads = out_weight.shape[0] // HD
    hidden_units = down_weight.shape[0]
    _, blocks, tokens, width = kv_cache.shape
    sources = reps * kvs
    sizes = (reps, kvs, tps, heads, blocks, tokens, rows, requests)
    vmem = pl.BlockSpec(memory_space=pltpu.VMEM)
    smem = pl.BlockSpec(memory_space=pltpu.SMEM)
    anywhere = pl.BlockSpec(memory_space=pl.ANY)
    dma = pltpu.SemaphoreType.DMA
    return pl.pallas_call(
        functools.partial(kernel, sizes),
        out_shape=(
            jax.ShapeDtypeStruct((1, rows, model), F32),
            jax.ShapeDtypeStruct((1, rows, width), F32),
        ),
        in_specs=[vmem] * 3 + [smem] * 5 + [anywhere] * 5,
        out_specs=(vmem, vmem),
        scratch_shapes=[
            pltpu.VMEM((width, model), BF16),
            pltpu.VMEM((width, model), BF16),
            pltpu.VMEM((width, model), BF16),
            pltpu.VMEM((hidden_units, model), BF16),
            pltpu.VMEM((hidden_units, model), BF16),
            pltpu.VMEM((blocks, tokens, width), BF16),
            pltpu.VMEM((kvs, rows, width), BF16),
            pltpu.VMEM((requests, width), F32),
            pltpu.VMEM((kvs, rows, 128), F32),
            pltpu.VMEM((kvs, rows, width), BF16),
            pltpu.VMEM((sources, rows, 128), F32),
            pltpu.VMEM((sources, rows, width), BF16),
            pltpu.VMEM((tps, rows, model), BF16),
            pltpu.VMEM((tps, rows, model), BF16),
            dma((4 * heads + 2,)),
            dma((blocks,)),
            dma((kvs,)),
            dma((kvs,)),
            dma((sources,)),
            dma((sources,)),
            dma((sources,)),
            dma((sources,)),
            dma((tps,)),
            dma((tps,)),
            dma((tps,)),
            dma((tps,)),
        ],
        compiler_params=pltpu.CompilerParams(
            collective_id=0, has_side_effects=True, vmem_limit_bytes=56 * 1024 * 1024
        ),
        name="decode_layer",
    )(
        token_state,
        attn_gain.reshape(1, model),
        mlp_gain.reshape(1, model),
        home_replica,
        moving,
        cache_length,
        block_owner,
        block_index,
        qkv_weight.T,
        out_weight,
        up_weight.T,
        down_weight,
        kv_cache,
    )


def solution(mesh):
    return jax.shard_map(
        functools.partial(body, mesh.shape["rep"], mesh.shape["kv"], mesh.shape["tp"]),
        mesh=mesh,
        in_specs=(
            P("kv", None),
            P(),
            P(None, "tp"),
            P("tp", None),
            P(),
            P(None, "tp"),
            P("tp", None),
            P("rep", "kv", None, "tp"),
            P(),
            P(),
            P(),
            P("rep", "kv"),
            P("rep", "kv"),
        ),
        out_specs=(P("rep", "kv", None), P("rep", "kv", "tp")),
        check_vma=False,
    )
```

```python
import functools

import jax
import jax.numpy as jnp
from jax import lax
from jax.experimental import pallas as pl
from jax.experimental.pallas import tpu as pltpu
from jax.sharding import PartitionSpec as P

HD = 80
PAIR = 2 * HD

very_low = -1e30
norm_eps = 1e-06

MESH = pl.DeviceIdType.MESH
BF16 = jnp.bfloat16
F32 = jnp.float32


def root_norm(values_in, gain_vector):
    values_in = values_in.astype(F32)
    scaled = values_in * lax.rsqrt(
        jnp.mean(values_in * values_in, axis=-1, keepdims=True) + norm_eps
    )
    return scaled * gain_vector


def gelu_tanh(x):
    return 0.5 * x * (1.0 + jnp.tanh(0.7978845608028654 * (x + 0.044715 * (x * x * x))))


def dot_last(left, right):
    return lax.dot_general(left, right, (((1,), (1,)), ((), ())), preferred_element_type=F32)


def dot_plain(left, right):
    return lax.dot_general(left, right, (((1,), (0,)), ((), ())), preferred_element_type=F32)


def kernel(
    sizes,
    state_ref,
    attn_gain_ref,
    mlp_gain_ref,
    home_ref,
    moving_ref,
    length_ref,
    owner_ref,
    index_ref,
    qkv_hbm,
    out_hbm,
    up_hbm,
    down_hbm,
    cache_hbm,
    hidden_ref,
    entries_ref,
    w_query,
    w_pair,
    w_out,
    w_up,
    w_down,
    cache,
    q_all,
    q_rows,
    stat_send,
    sums_send,
    stat_recv,
    sums_recv,
    part_out,
    part_down,
    load_sem,
    cache_sem,
    q_send_sem,
    q_recv_sem,
    stat_send_sem,
    stat_recv_sem,
    sums_send_sem,
    sums_recv_sem,
    out_send_sem,
    out_recv_sem,
    down_send_sem,
    down_recv_sem,
):
    reps, kvs, tps, heads, blocks, tokens, rows, requests = sizes
    width = heads * PAIR
    sources = reps * kvs
    rep = lax.axis_index("rep")
    kv = lax.axis_index("kv")
    tp = lax.axis_index("tp")
    me = rep * kvs + kv

    def source_id(number):
        return {"rep": lax.div(number, kvs), "kv": lax.rem(number, kvs)}

    barrier = pltpu.get_barrier_semaphore()
    for step in range(1, sources):
        pl.semaphore_signal(
            barrier,
            inc=1,
            device_id=source_id(lax.rem(me + step, sources)),
            device_id_type=MESH,
        )
    for step in range(1, tps):
        pl.semaphore_signal(
            barrier, inc=1, device_id={"tp": lax.rem(tp + step, tps)}, device_id_type=MESH
        )

    query_loads, pair_loads = [], []
    for h in range(heads):
        query_loads.append(
            pltpu.make_async_copy(
                qkv_hbm.at[pl.ds(h * 3 * HD, HD)],
                w_query.at[pl.ds(h * HD, HD)],
                load_sem.at[h],
            )
        )
        pair_loads.append(
            pltpu.make_async_copy(
                qkv_hbm.at[pl.ds(h * 3 * HD + HD, PAIR)],
                w_pair.at[pl.ds(h * PAIR, PAIR)],
                load_sem.at[heads + h],
            )
        )
    out_load = pltpu.make_async_copy(out_hbm, w_out, load_sem.at[2 * heads])
    up_load = pltpu.make_async_copy(up_hbm, w_up, load_sem.at[2 * heads + 1])
    down_load = pltpu.make_async_copy(down_hbm, w_down, load_sem.at[2 * heads + 2])
    cache_loads = [
        pltpu.make_async_copy(cache_hbm.at[0, b], cache.at[b], cache_sem.at[b])
        for b in range(blocks)
    ]
    for copy in query_loads + cache_loads + pair_loads + [out_load, up_load, down_load]:
        copy.start()

    state = state_ref[...].astype(F32)
    normed = root_norm(state, attn_gain_ref[...].reshape(1, -1)).astype(BF16)
    for copy in query_loads:
        copy.wait()
    compact = dot_last(normed, w_query[...]) * HD ** (-0.5)
    gap = jnp.zeros((rows, HD), F32)
    spread = []
    for h in range(heads):
        spread += [compact[:, h * HD : (h + 1) * HD], gap]
    query = jnp.concatenate(spread, axis=1).astype(BF16)
    q_all[kv] = query

    pl.semaphore_wait(barrier, sources - 1 + tps - 1)

    q_sends = []
    for step in range(1, kvs):
        copy = pltpu.make_async_remote_copy(
            src_ref=q_all.at[kv],
            dst_ref=q_all.at[kv],
            send_sem=q_send_sem.at[step],
            recv_sem=q_recv_sem.at[kv],
            device_id={"kv": lax.rem(kv + step, kvs)},
            device_id_type=MESH,
        )
        copy.start()
        q_sends.append(copy)

    for copy in pair_loads:
        copy.wait()
    pairs = dot_last(normed, w_pair[...])
    fresh = pairs.astype(BF16).astype(F32)
    lane = lax.broadcasted_iota(jnp.int32, (1, width), 1)
    lane_head = sum((lane >= h * PAIR).astype(jnp.int32) for h in range(1, heads))
    is_value = (lane - lane_head * PAIR) >= HD
    small_lane = lax.broadcasted_iota(jnp.int32, (1, 128), 1)
    self_products = jnp.where(is_value, 0.0, query.astype(F32) * fresh)
    self_score = jnp.full((rows, 128), very_low, F32)
    for h in range(heads):
        score = jnp.sum(jnp.where(lane_head == h, self_products, 0.0), axis=1, keepdims=True)
        self_score = jnp.where(small_lane == h, score, self_score)
    fresh_values = jnp.where(is_value, fresh, 0.0)

    row_number = lax.broadcasted_iota(jnp.int32, (rows, 1), 0)
    target = jnp.zeros((rows, 1), jnp.int32)
    for i in range(rows):
        slot = kv * rows + i
        aim = jnp.bitwise_xor(home_ref[slot], moving_ref[slot])
        target = jnp.where(row_number == i, aim, target)
    served_here = target == rep
    entries_ref[0] = jnp.where(served_here, pairs, 0.0)

    for step in range(1, kvs):
        other = lax.rem(kv + step, kvs)
        pltpu.make_async_remote_copy(
            src_ref=q_all.at[other],
            dst_ref=q_all.at[other],
            send_sem=q_send_sem.at[step],
            recv_sem=q_recv_sem.at[other],
            device_id={"kv": other},
            device_id_type=MESH,
        ).wait_recv()
    q_rows[...] = q_all[...].astype(F32).reshape(requests, width)

    head_row = lax.broadcasted_iota(jnp.int32, (8, 1), 0)
    key_mask = (lane_head == head_row) & ~is_value
    value_mask = (lane_head == head_row) & is_value
    token_lane = lax.broadcasted_iota(jnp.int32, (1, tokens), 1)

    for copy in cache_loads:
        copy.wait()
    owners, limits, scores, peaks = [], [], [], []
    for b in range(blocks):
        owner = owner_ref[0, b]
        clipped = jnp.minimum(owner, requests - 1)
        limit = jnp.where(
            owner < requests, length_ref[clipped] - index_ref[0, b] * tokens, 0
        )
        q_row = q_rows[pl.ds(clipped, 1), :]
        block_query = jnp.where(key_mask, q_row, 0.0).astype(BF16)
        score = dot_last(block_query, cache[b])
        score = jnp.where(token_lane < limit, score, very_low)
        owners.append(owner)
        limits.append(limit)
        scores.append(score)
        peaks.append(jnp.max(score, axis=1, keepdims=True))

    slot_row = lax.broadcasted_iota(jnp.int32, (requests, 1), 0)
    sums = jnp.zeros((requests, width), F32)
    stats = jnp.where(small_lane < 8, very_low, 0.0) + jnp.zeros((requests, 128), F32)
    for b in range(blocks):
        shift = peaks[b]
        for other in range(blocks):
            if other != b:
                shift = jnp.where(
                    owners[other] == owners[b], jnp.maximum(shift, peaks[other]), shift
                )
        weight = jnp.where(token_lane < limits[b], jnp.exp(scores[b] - shift), 0.0)
        total = jnp.sum(weight, axis=1, keepdims=True)
        acc = dot_plain(weight.astype(BF16), cache[b])
        acc_row = jnp.sum(jnp.where(value_mask, acc, 0.0), axis=0, keepdims=True)
        stat_row = jnp.sum(
            jnp.where(
                small_lane == head_row, shift, jnp.where(small_lane == head_row + 8, total, 0.0)
            ),
            axis=0,
            keepdims=True,
        )
        mine = slot_row == owners[b]
        sums = sums + jnp.where(mine, acc_row, 0.0)
        stats = jnp.where(
            mine, jnp.where(small_lane < 8, stat_row, stats + stat_row), stats
        )
    stat_send[...] = stats.reshape(kvs, rows, 128)
    sums_send[...] = sums.reshape(kvs, rows, width).astype(BF16)

    partial_sends = []
    for step in range(1, sources):
        to = lax.rem(me + step, sources)
        to_kv = lax.rem(to, kvs)
        for src, dst, send_sem, recv_sem in (
            (stat_send, stat_recv, stat_send_sem, stat_recv_sem),
            (sums_send, sums_recv, sums_send_sem, sums_recv_sem),
        ):
            copy = pltpu.make_async_remote_copy(
                src_ref=src.at[to_kv],
                dst_ref=dst.at[me],
                send_sem=send_sem.at[step],
                recv_sem=recv_sem.at[me],
                device_id=source_id(to),
                device_id_type=MESH,
            )
            copy.start()
            partial_sends.append(copy)
    stat_recv[me] = stat_send[kv]
    sums_recv[me] = sums_send[kv]
    for step in range(1, sources):
        other = lax.rem(me + step, sources)
        for dst, send_sem, recv_sem in (
            (stat_recv, stat_send_sem, stat_recv_sem),
            (sums_recv, sums_send_sem, sums_recv_sem),
        ):
            pltpu.make_async_remote_copy(
                src_ref=dst.at[other],
                dst_ref=dst.at[other],
                send_sem=send_sem.at[step],
                recv_sem=recv_sem.at[other],
                device_id=source_id(other),
                device_id_type=MESH,
            ).wait_recv()

    def over_lanes(values):
        wide = jnp.broadcast_to(values[:, heads - 1 : heads], (rows, width))
        for h in reversed(range(heads - 1)):
            wide = jnp.where(lane < (h + 1) * PAIR, values[:, h : h + 1], wide)
        return wide

    top = self_score
    for s in range(sources):
        top = jnp.maximum(top, stat_recv[s])
    in_heads = small_lane < heads
    self_weight = jnp.exp(self_score - top)
    denominator = self_weight
    factors = []
    for s in range(sources):
        stat = stat_recv[s]
        factor = jnp.exp(stat - top)
        factors.append(factor)
        denominator = denominator + pltpu.roll(stat, 120, 1) * factor
    denominator = jnp.where(in_heads, denominator, 1.0)
    numerator = over_lanes(self_weight.astype(BF16).astype(F32)) * fresh_values
    for s in range(sources):
        numerator = numerator + over_lanes(factors[s]) * sums_recv[s].astype(F32)
    attended = numerator / over_lanes(denominator)
    attended = jnp.concatenate(
        [attended[:, h * PAIR + HD : (h + 1) * PAIR] for h in range(heads)], axis=1
    ).astype(BF16)

    def summed_over_tp(part, buffer, send_sem, recv_sem):
        buffer[tp] = part.astype(BF16)
        sends = []
        for step in range(1, tps):
            copy = pltpu.make_async_remote_copy(
                src_ref=buffer.at[tp],
                dst_ref=buffer.at[tp],
                send_sem=send_sem.at[step],
                recv_sem=recv_sem.at[tp],
                device_id={"tp": lax.rem(tp + step, tps)},
                device_id_type=MESH,
            )
            copy.start()
            sends.append(copy)
        for step in range(1, tps):
            other = lax.rem(tp + step, tps)
            pltpu.make_async_remote_copy(
                src_ref=buffer.at[other],
                dst_ref=buffer.at[other],
                send_sem=send_sem.at[step],
                recv_sem=recv_sem.at[other],
                device_id={"tp": other},
                device_id_type=MESH,
            ).wait_recv()
        total = buffer[0].astype(F32)
        for t in range(1, tps):
            total = total + buffer[t].astype(F32)
        return total, sends

    out_load.wait()
    attn_out, out_sends = summed_over_tp(
        dot_plain(attended, w_out[...]), part_out, out_send_sem, out_recv_sem
    )
    residual = state + attn_out
    normed_mlp = root_norm(residual, mlp_gain_ref[...].reshape(1, -1)).astype(BF16)
    up_load.wait()
    activated = gelu_tanh(dot_last(normed_mlp, w_up[...])).astype(BF16)
    down_load.wait()
    mlp_out, down_sends = summed_over_tp(
        dot_plain(activated, w_down[...]), part_down, down_send_sem, down_recv_sem
    )
    hidden_ref[0] = jnp.where(served_here, residual + mlp_out, 0.0)
    for copy in q_sends + partial_sends + out_sends + down_sends:
        copy.wait_send()


def body(
    reps,
    kvs,
    tps,
    token_state,
    attn_gain,
    qkv_weight,
    out_weight,
    mlp_gain,
    up_weight,
    down_weight,
    kv_cache,
    home_replica,
    moving,
    cache_length,
    block_owner,
    block_index,
):
    rows, model = token_state.shape
    requests = home_replica.shape[0]
    heads = out_weight.shape[0] // HD
    hidden_units = down_weight.shape[0]
    _, blocks, tokens, width = kv_cache.shape
    sources = reps * kvs
    sizes = (reps, kvs, tps, heads, blocks, tokens, rows, requests)
    vmem = pl.BlockSpec(memory_space=pltpu.VMEM)
    smem = pl.BlockSpec(memory_space=pltpu.SMEM)
    anywhere = pl.BlockSpec(memory_space=pl.ANY)
    dma = pltpu.SemaphoreType.DMA
    return pl.pallas_call(
        functools.partial(kernel, sizes),
        out_shape=(
            pltpu.VMEM((1, rows, model), F32),
            pltpu.VMEM((1, rows, width), F32),
        ),
        in_specs=[vmem] * 3 + [smem] * 5 + [anywhere] * 5,
        out_specs=(vmem, vmem),
        scratch_shapes=[
            pltpu.VMEM((heads * HD, model), BF16),
            pltpu.VMEM((width, model), BF16),
            pltpu.VMEM((heads * HD, model), BF16),
            pltpu.VMEM((hidden_units, model), BF16),
            pltpu.VMEM((hidden_units, model), BF16),
            pltpu.VMEM((blocks, tokens, width), BF16),
            pltpu.VMEM((kvs, rows, width), BF16),
            pltpu.VMEM((requests, width), F32),
            pltpu.VMEM((kvs, rows, 128), F32),
            pltpu.VMEM((kvs, rows, width), BF16),
            pltpu.VMEM((sources, rows, 128), F32),
            pltpu.VMEM((sources, rows, width), BF16),
            pltpu.VMEM((tps, rows, model), BF16),
            pltpu.VMEM((tps, rows, model), BF16),
            dma((2 * heads + 3,)),
            dma((blocks,)),
            dma((kvs,)),
            dma((kvs,)),
            dma((sources,)),
            dma((sources,)),
            dma((sources,)),
            dma((sources,)),
            dma((tps,)),
            dma((tps,)),
            dma((tps,)),
            dma((tps,)),
        ],
        compiler_params=pltpu.CompilerParams(
            collective_id=0, has_side_effects=True, vmem_limit_bytes=56 * 1024 * 1024
        ),
        name="decode_layer",
    )(
        token_state,
        attn_gain,
        mlp_gain,
        home_replica,
        moving,
        cache_length,
        block_owner,
        block_index,
        qkv_weight.T,
        out_weight,
        up_weight.T,
        down_weight,
        kv_cache,
    )


def solution(mesh):
    return jax.shard_map(
        functools.partial(body, mesh.shape["rep"], mesh.shape["kv"], mesh.shape["tp"]),
        mesh=mesh,
        in_specs=(
            P("kv", None),
            P(),
            P(None, "tp"),
            P("tp", None),
            P(),
            P(None, "tp"),
            P("tp", None),
            P("rep", "kv", None, "tp"),
            P(),
            P(),
            P(),
            P("rep", "kv"),
            P("rep", "kv"),
        ),
        out_specs=(P("rep", "kv", None), P("rep", "kv", "tp")),
        check_vma=False,
    )
```

```python
import functools

import jax
import jax.numpy as jnp
from jax import lax
from jax.experimental import pallas as pl
from jax.experimental.pallas import tpu as pltpu
from jax.sharding import PartitionSpec as P

HD = 80
PAIR = 2 * HD

very_low = -1e30
norm_eps = 1e-06

MESH = pl.DeviceIdType.MESH
BF16 = jnp.bfloat16
F32 = jnp.float32


def root_norm(values_in, gain_vector):
    values_in = values_in.astype(F32)
    scaled = values_in * lax.rsqrt(
        jnp.mean(values_in * values_in, axis=-1, keepdims=True) + norm_eps
    )
    return scaled * gain_vector


def gelu_tanh(x):
    return 0.5 * x * (1.0 + jnp.tanh(0.7978845608028654 * (x + 0.044715 * (x * x * x))))


def dot_last(left, right):
    return lax.dot_general(left, right, (((1,), (1,)), ((), ())), preferred_element_type=F32)


def dot_plain(left, right):
    return lax.dot_general(left, right, (((1,), (0,)), ((), ())), preferred_element_type=F32)


def kernel(
    sizes,
    state_hbm,
    attn_gain_hbm,
    mlp_gain_hbm,
    home_hbm,
    moving_hbm,
    length_hbm,
    owner_hbm,
    index_hbm,
    qkv_hbm,
    out_hbm,
    up_hbm,
    down_hbm,
    cache_hbm,
    hidden_ref,
    entries_ref,
    state_ref,
    attn_gain_ref,
    mlp_gain_ref,
    home_ref,
    moving_ref,
    length_ref,
    owner_ref,
    index_ref,
    w_query,
    w_pair,
    w_out,
    w_up,
    w_down,
    cache,
    q_all,
    q_rows,
    stat_send,
    sums_send,
    stat_recv,
    sums_recv,
    part_out,
    part_down,
    small_sem,
    load_sem,
    cache_sem,
    q_send_sem,
    q_recv_sem,
    stat_send_sem,
    stat_recv_sem,
    sums_send_sem,
    sums_recv_sem,
    out_send_sem,
    out_recv_sem,
    down_send_sem,
    down_recv_sem,
):
    reps, kvs, tps, heads, blocks, tokens, rows, requests = sizes
    width = heads * PAIR
    sources = reps * kvs
    rep = lax.axis_index("rep")
    kv = lax.axis_index("kv")
    tp = lax.axis_index("tp")
    me = rep * kvs + kv

    def source_id(number):
        return {"rep": lax.div(number, kvs), "kv": lax.rem(number, kvs)}

    barrier = pltpu.get_barrier_semaphore()
    for step in range(1, sources):
        pl.semaphore_signal(
            barrier,
            inc=1,
            device_id=source_id(lax.rem(me + step, sources)),
            device_id_type=MESH,
        )
    for step in range(1, tps):
        pl.semaphore_signal(
            barrier, inc=1, device_id={"tp": lax.rem(tp + step, tps)}, device_id_type=MESH
        )

    small_loads = [
        pltpu.make_async_copy(source, held, small_sem.at[i])
        for i, (source, held) in enumerate(
            (
                (state_hbm, state_ref),
                (attn_gain_hbm, attn_gain_ref),
                (mlp_gain_hbm, mlp_gain_ref),
                (home_hbm, home_ref),
                (moving_hbm, moving_ref),
                (length_hbm, length_ref),
                (owner_hbm, owner_ref),
                (index_hbm, index_ref),
            )
        )
    ]
    query_loads, pair_loads = [], []
    for h in range(heads):
        query_loads.append(
            pltpu.make_async_copy(
                qkv_hbm.at[pl.ds(h * 3 * HD, HD)],
                w_query.at[pl.ds(h * HD, HD)],
                load_sem.at[h],
            )
        )
        pair_loads.append(
            pltpu.make_async_copy(
                qkv_hbm.at[pl.ds(h * 3 * HD + HD, PAIR)],
                w_pair.at[pl.ds(h * PAIR, PAIR)],
                load_sem.at[heads + h],
            )
        )
    out_load = pltpu.make_async_copy(out_hbm, w_out, load_sem.at[2 * heads])
    up_load = pltpu.make_async_copy(up_hbm, w_up, load_sem.at[2 * heads + 1])
    down_load = pltpu.make_async_copy(down_hbm, w_down, load_sem.at[2 * heads + 2])
    cache_loads = [
        pltpu.make_async_copy(cache_hbm.at[0, b], cache.at[b], cache_sem.at[b])
        for b in range(blocks)
    ]
    for copy in small_loads[:2] + query_loads + small_loads[2:] + cache_loads:
        copy.start()
    for copy in pair_loads + [out_load, up_load, down_load]:
        copy.start()
    for copy in small_loads[:2]:
        copy.wait()

    state = state_ref[...].astype(F32)
    normed = root_norm(state, attn_gain_ref[...].reshape(1, -1)).astype(BF16)
    for copy in query_loads:
        copy.wait()
    compact = dot_last(normed, w_query[...]) * HD ** (-0.5)
    gap = jnp.zeros((rows, HD), F32)
    spread = []
    for h in range(heads):
        spread += [compact[:, h * HD : (h + 1) * HD], gap]
    query = jnp.concatenate(spread, axis=1).astype(BF16)
    q_all[kv] = query

    pl.semaphore_wait(barrier, sources - 1 + tps - 1)

    q_sends = []
    for step in range(1, kvs):
        copy = pltpu.make_async_remote_copy(
            src_ref=q_all.at[kv],
            dst_ref=q_all.at[kv],
            send_sem=q_send_sem.at[step],
            recv_sem=q_recv_sem.at[kv],
            device_id={"kv": lax.rem(kv + step, kvs)},
            device_id_type=MESH,
        )
        copy.start()
        q_sends.append(copy)

    lane = lax.broadcasted_iota(jnp.int32, (1, width), 1)
    lane_head = sum((lane >= h * PAIR).astype(jnp.int32) for h in range(1, heads))
    is_value = (lane - lane_head * PAIR) >= HD
    small_lane = lax.broadcasted_iota(jnp.int32, (1, 128), 1)
    for copy in small_loads[2:]:
        copy.wait()
    for step in range(1, kvs):
        other = lax.rem(kv + step, kvs)
        pltpu.make_async_remote_copy(
            src_ref=q_all.at[other],
            dst_ref=q_all.at[other],
            send_sem=q_send_sem.at[step],
            recv_sem=q_recv_sem.at[other],
            device_id={"kv": other},
            device_id_type=MESH,
        ).wait_recv()
    q_rows[...] = q_all[...].astype(F32).reshape(requests, width)

    head_row = lax.broadcasted_iota(jnp.int32, (8, 1), 0)
    key_mask = (lane_head == head_row) & ~is_value
    value_mask = (lane_head == head_row) & is_value
    token_lane = lax.broadcasted_iota(jnp.int32, (1, tokens), 1)

    for copy in cache_loads:
        copy.wait()
    owners, limits, scores, peaks = [], [], [], []
    for b in range(blocks):
        owner = owner_ref[0, b]
        clipped = jnp.minimum(owner, requests - 1)
        limit = jnp.where(
            owner < requests, length_ref[clipped] - index_ref[0, b] * tokens, 0
        )
        q_row = q_rows[pl.ds(clipped, 1), :]
        block_query = jnp.where(key_mask, q_row, 0.0).astype(BF16)
        score = dot_last(block_query, cache[b])
        score = jnp.where(token_lane < limit, score, very_low)
        owners.append(owner)
        limits.append(limit)
        scores.append(score)
        peaks.append(jnp.max(score, axis=1, keepdims=True))

    slot_row = lax.broadcasted_iota(jnp.int32, (requests, 1), 0)
    sums = jnp.zeros((requests, width), F32)
    stats = jnp.where(small_lane < 8, very_low, 0.0) + jnp.zeros((requests, 128), F32)
    for b in range(blocks):
        shift = peaks[b]
        for other in range(blocks):
            if other != b:
                shift = jnp.where(
                    owners[other] == owners[b], jnp.maximum(shift, peaks[other]), shift
                )
        weight = jnp.where(token_lane < limits[b], jnp.exp(scores[b] - shift), 0.0)
        total = jnp.sum(weight, axis=1, keepdims=True)
        acc = dot_plain(weight.astype(BF16), cache[b])
        acc_row = jnp.sum(jnp.where(value_mask, acc, 0.0), axis=0, keepdims=True)
        stat_row = jnp.sum(
            jnp.where(
                small_lane == head_row, shift, jnp.where(small_lane == head_row + 8, total, 0.0)
            ),
            axis=0,
            keepdims=True,
        )
        mine = slot_row == owners[b]
        sums = sums + jnp.where(mine, acc_row, 0.0)
        stats = jnp.where(
            mine, jnp.where(small_lane < 8, stat_row, stats + stat_row), stats
        )
    stat_send[...] = stats.reshape(kvs, rows, 128)
    sums_send[...] = sums.reshape(kvs, rows, width).astype(BF16)

    partial_sends = []
    for step in range(1, sources):
        to = lax.rem(me + step, sources)
        to_kv = lax.rem(to, kvs)
        for src, dst, send_sem, recv_sem in (
            (stat_send, stat_recv, stat_send_sem, stat_recv_sem),
            (sums_send, sums_recv, sums_send_sem, sums_recv_sem),
        ):
            copy = pltpu.make_async_remote_copy(
                src_ref=src.at[to_kv],
                dst_ref=dst.at[me],
                send_sem=send_sem.at[step],
                recv_sem=recv_sem.at[me],
                device_id=source_id(to),
                device_id_type=MESH,
            )
            copy.start()
            partial_sends.append(copy)
    stat_recv[me] = stat_send[kv]
    sums_recv[me] = sums_send[kv]

    for copy in pair_loads:
        copy.wait()
    pairs = dot_last(normed, w_pair[...])
    fresh = pairs.astype(BF16).astype(F32)
    self_products = jnp.where(is_value, 0.0, query.astype(F32) * fresh)
    self_score = jnp.full((rows, 128), very_low, F32)
    for h in range(heads):
        score = jnp.sum(jnp.where(lane_head == h, self_products, 0.0), axis=1, keepdims=True)
        self_score = jnp.where(small_lane == h, score, self_score)
    fresh_values = jnp.where(is_value, fresh, 0.0)

    row_number = lax.broadcasted_iota(jnp.int32, (rows, 1), 0)
    target = jnp.zeros((rows, 1), jnp.int32)
    for i in range(rows):
        slot = kv * rows + i
        aim = jnp.bitwise_xor(home_ref[slot], moving_ref[slot])
        target = jnp.where(row_number == i, aim, target)
    served_here = target == rep
    entries_ref[0] = jnp.where(served_here, pairs, 0.0)

    for step in range(1, sources):
        other = lax.rem(me + step, sources)
        for dst, send_sem, recv_sem in (
            (stat_recv, stat_send_sem, stat_recv_sem),
            (sums_recv, sums_send_sem, sums_recv_sem),
        ):
            pltpu.make_async_remote_copy(
                src_ref=dst.at[other],
                dst_ref=dst.at[other],
                send_sem=send_sem.at[step],
                recv_sem=recv_sem.at[other],
                device_id=source_id(other),
                device_id_type=MESH,
            ).wait_recv()

    def over_lanes(values):
        wide = jnp.broadcast_to(values[:, heads - 1 : heads], (rows, width))
        for h in reversed(range(heads - 1)):
            wide = jnp.where(lane < (h + 1) * PAIR, values[:, h : h + 1], wide)
        return wide

    top = self_score
    for s in range(sources):
        top = jnp.maximum(top, stat_recv[s])
    in_heads = small_lane < heads
    self_weight = jnp.exp(self_score - top)
    denominator = self_weight
    factors = []
    for s in range(sources):
        stat = stat_recv[s]
        factor = jnp.exp(stat - top)
        factors.append(factor)
        denominator = denominator + pltpu.roll(stat, 120, 1) * factor
    denominator = jnp.where(in_heads, denominator, 1.0)
    numerator = over_lanes(self_weight.astype(BF16).astype(F32)) * fresh_values
    for s in range(sources):
        numerator = numerator + over_lanes(factors[s]) * sums_recv[s].astype(F32)
    attended = numerator / over_lanes(denominator)
    attended = jnp.concatenate(
        [attended[:, h * PAIR + HD : (h + 1) * PAIR] for h in range(heads)], axis=1
    ).astype(BF16)

    def summed_over_tp(part, buffer, send_sem, recv_sem):
        buffer[tp] = part.astype(BF16)
        sends = []
        for step in range(1, tps):
            copy = pltpu.make_async_remote_copy(
                src_ref=buffer.at[tp],
                dst_ref=buffer.at[tp],
                send_sem=send_sem.at[step],
                recv_sem=recv_sem.at[tp],
                device_id={"tp": lax.rem(tp + step, tps)},
                device_id_type=MESH,
            )
            copy.start()
            sends.append(copy)
        for step in range(1, tps):
            other = lax.rem(tp + step, tps)
            pltpu.make_async_remote_copy(
                src_ref=buffer.at[other],
                dst_ref=buffer.at[other],
                send_sem=send_sem.at[step],
                recv_sem=recv_sem.at[other],
                device_id={"tp": other},
                device_id_type=MESH,
            ).wait_recv()
        total = buffer[0].astype(F32)
        for t in range(1, tps):
            total = total + buffer[t].astype(F32)
        return total, sends

    out_load.wait()
    attn_out, out_sends = summed_over_tp(
        dot_plain(attended, w_out[...]), part_out, out_send_sem, out_recv_sem
    )
    residual = state + attn_out
    normed_mlp = root_norm(residual, mlp_gain_ref[...].reshape(1, -1)).astype(BF16)
    up_load.wait()
    activated = gelu_tanh(dot_last(normed_mlp, w_up[...])).astype(BF16)
    down_load.wait()
    mlp_out, down_sends = summed_over_tp(
        dot_plain(activated, w_down[...]), part_down, down_send_sem, down_recv_sem
    )
    hidden_ref[0] = jnp.where(served_here, residual + mlp_out, 0.0)
    for copy in q_sends + partial_sends + out_sends + down_sends:
        copy.wait_send()


def write_results(hidden_in, entries_in, hidden_out, entries_out, sem):
    copies = [
        pltpu.make_async_copy(hidden_in, hidden_out, sem.at[0]),
        pltpu.make_async_copy(entries_in, entries_out, sem.at[1]),
    ]
    for copy in copies:
        copy.start()
    for copy in copies:
        copy.wait()


def body(
    reps,
    kvs,
    tps,
    token_state,
    attn_gain,
    qkv_weight,
    out_weight,
    mlp_gain,
    up_weight,
    down_weight,
    kv_cache,
    home_replica,
    moving,
    cache_length,
    block_owner,
    block_index,
):
    rows, model = token_state.shape
    requests = home_replica.shape[0]
    heads = out_weight.shape[0] // HD
    hidden_units = down_weight.shape[0]
    _, blocks, tokens, width = kv_cache.shape
    sources = reps * kvs
    sizes = (reps, kvs, tps, heads, blocks, tokens, rows, requests)
    vmem = pl.BlockSpec(memory_space=pltpu.VMEM)
    anywhere = pl.BlockSpec(memory_space=pl.ANY)
    dma = pltpu.SemaphoreType.DMA
    results = pl.pallas_call(
        functools.partial(kernel, sizes),
        out_shape=(
            pltpu.VMEM((1, rows, model), F32),
            pltpu.VMEM((1, rows, width), F32),
        ),
        in_specs=[anywhere] * 13,
        out_specs=(vmem, vmem),
        scratch_shapes=[
            pltpu.VMEM((rows, model), BF16),
            pltpu.VMEM((model,), F32),
            pltpu.VMEM((model,), F32),
            pltpu.SMEM((requests,), jnp.int32),
            pltpu.SMEM((requests,), jnp.int32),
            pltpu.SMEM((requests,), jnp.int32),
            pltpu.SMEM((1, blocks), jnp.int32),
            pltpu.SMEM((1, blocks), jnp.int32),
            pltpu.VMEM((heads * HD, model), BF16),
            pltpu.VMEM((width, model), BF16),
            pltpu.VMEM((heads * HD, model), BF16),
            pltpu.VMEM((hidden_units, model), BF16),
            pltpu.VMEM((hidden_units, model), BF16),
            pltpu.VMEM((blocks, tokens, width), BF16),
            pltpu.VMEM((kvs, rows, width), BF16),
            pltpu.VMEM((requests, width), F32),
            pltpu.VMEM((kvs, rows, 128), F32),
            pltpu.VMEM((kvs, rows, width), BF16),
            pltpu.VMEM((sources, rows, 128), F32),
            pltpu.VMEM((sources, rows, width), BF16),
            pltpu.VMEM((tps, rows, model), BF16),
            pltpu.VMEM((tps, rows, model), BF16),
            dma((8,)),
            dma((2 * heads + 3,)),
            dma((blocks,)),
            dma((kvs,)),
            dma((kvs,)),
            dma((sources,)),
            dma((sources,)),
            dma((sources,)),
            dma((sources,)),
            dma((tps,)),
            dma((tps,)),
            dma((tps,)),
            dma((tps,)),
        ],
        compiler_params=pltpu.CompilerParams(
            collective_id=0, has_side_effects=True, vmem_limit_bytes=56 * 1024 * 1024
        ),
        name="decode_layer",
    )(
        token_state,
        attn_gain,
        mlp_gain,
        home_replica,
        moving,
        cache_length,
        block_owner,
        block_index,
        qkv_weight.T,
        out_weight,
        up_weight.T,
        down_weight,
        kv_cache,
    )
    return pl.pallas_call(
        write_results,
        out_shape=(
            jax.ShapeDtypeStruct((1, rows, model), F32),
            jax.ShapeDtypeStruct((1, rows, width), F32),
        ),
        in_specs=[vmem] * 2,
        out_specs=(anywhere, anywhere),
        scratch_shapes=[dma((2,))],
        name="write_results",
    )(*results)


def solution(mesh):
    return jax.shard_map(
        functools.partial(body, mesh.shape["rep"], mesh.shape["kv"], mesh.shape["tp"]),
        mesh=mesh,
        in_specs=(
            P("kv", None),
            P(),
            P(None, "tp"),
            P("tp", None),
            P(),
            P(None, "tp"),
            P("tp", None),
            P("rep", "kv", None, "tp"),
            P(),
            P(),
            P(),
            P("rep", "kv"),
            P("rep", "kv"),
        ),
        out_specs=(P("rep", "kv", None), P("rep", "kv", "tp")),
        check_vma=False,
    )
```

```python
import functools

import jax
import jax.numpy as jnp
from jax import lax
from jax.experimental import pallas as pl
from jax.experimental.pallas import tpu as pltpu
from jax.sharding import PartitionSpec as P

HD = 80
PAIR = 2 * HD

very_low = -1e30
norm_eps = 1e-06

MESH = pl.DeviceIdType.MESH
BF16 = jnp.bfloat16
F32 = jnp.float32


def root_norm(values_in, gain_vector):
    values_in = values_in.astype(F32)
    scaled = values_in * lax.rsqrt(
        jnp.mean(values_in * values_in, axis=-1, keepdims=True) + norm_eps
    )
    return scaled * gain_vector


def gelu_tanh(x):
    return 0.5 * x * (1.0 + jnp.tanh(0.7978845608028654 * (x + 0.044715 * (x * x * x))))


def dot_last(left, right):
    return lax.dot_general(left, right, (((1,), (1,)), ((), ())), preferred_element_type=F32)


def dot_plain(left, right):
    return lax.dot_general(left, right, (((1,), (0,)), ((), ())), preferred_element_type=F32)


def kernel(
    sizes,
    state_hbm,
    attn_gain_hbm,
    mlp_gain_hbm,
    home_hbm,
    moving_hbm,
    length_hbm,
    owner_hbm,
    index_hbm,
    qkv_hbm,
    out_hbm,
    up_hbm,
    down_hbm,
    cache_hbm,
    hidden_ref,
    entries_ref,
    state_ref,
    attn_gain_ref,
    mlp_gain_ref,
    home_ref,
    moving_ref,
    length_ref,
    owner_ref,
    index_ref,
    w_query,
    w_pair,
    w_out,
    w_up,
    w_down,
    cache,
    q_all,
    q_rows,
    stat_send,
    sums_send,
    stat_recv,
    sums_recv,
    part_out,
    part_down,
    small_sem,
    load_sem,
    cache_sem,
    q_send_sem,
    q_recv_sem,
    stat_send_sem,
    stat_recv_sem,
    sums_send_sem,
    sums_recv_sem,
    out_send_sem,
    out_recv_sem,
    down_send_sem,
    down_recv_sem,
):
    reps, kvs, tps, heads, blocks, tokens, rows, requests = sizes
    width = heads * PAIR
    sources = reps * kvs
    rep = lax.axis_index("rep")
    kv = lax.axis_index("kv")
    tp = lax.axis_index("tp")
    me = rep * kvs + kv

    def source_id(number):
        return {"rep": lax.div(number, kvs), "kv": lax.rem(number, kvs)}

    barrier = pltpu.get_barrier_semaphore()
    for step in range(1, sources):
        pl.semaphore_signal(
            barrier,
            inc=1,
            device_id=source_id(lax.rem(me + step, sources)),
            device_id_type=MESH,
        )
    for step in range(1, tps):
        pl.semaphore_signal(
            barrier, inc=1, device_id={"tp": lax.rem(tp + step, tps)}, device_id_type=MESH
        )

    small_loads = [
        pltpu.make_async_copy(source, held, small_sem.at[i])
        for i, (source, held) in enumerate(
            (
                (state_hbm, state_ref),
                (attn_gain_hbm, attn_gain_ref),
                (mlp_gain_hbm, mlp_gain_ref),
                (home_hbm, home_ref),
                (moving_hbm, moving_ref),
                (length_hbm, length_ref),
                (owner_hbm, owner_ref),
                (index_hbm, index_ref),
            )
        )
    ]
    query_loads, pair_loads = [], []
    for h in range(heads):
        query_loads.append(
            pltpu.make_async_copy(
                qkv_hbm.at[pl.ds(h * 3 * HD, HD)],
                w_query.at[pl.ds(h * HD, HD)],
                load_sem.at[h],
            )
        )
        pair_loads.append(
            pltpu.make_async_copy(
                qkv_hbm.at[pl.ds(h * 3 * HD + HD, PAIR)],
                w_pair.at[pl.ds(h * PAIR, PAIR)],
                load_sem.at[heads + h],
            )
        )
    out_load = pltpu.make_async_copy(out_hbm, w_out, load_sem.at[2 * heads])
    up_load = pltpu.make_async_copy(up_hbm, w_up, load_sem.at[2 * heads + 1])
    down_load = pltpu.make_async_copy(down_hbm, w_down, load_sem.at[2 * heads + 2])
    middle = (blocks + 1) // 2
    cache_loads = [
        pltpu.make_async_copy(
            cache_hbm.at[0, pl.ds(first, count)], cache.at[pl.ds(first, count)], cache_sem.at[i]
        )
        for i, (first, count) in enumerate(((0, middle), (middle, blocks - middle)))
    ]
    for copy in small_loads[:2] + query_loads + cache_loads:
        copy.start()
    for copy in small_loads[:2]:
        copy.wait()

    state = state_ref[...].astype(F32)
    normed = root_norm(state, attn_gain_ref[...].reshape(1, -1)).astype(BF16)
    for copy in query_loads:
        copy.wait()
    compact = dot_last(normed, w_query[...]) * HD ** (-0.5)
    gap = jnp.zeros((rows, HD), F32)
    spread = []
    for h in range(heads):
        spread += [compact[:, h * HD : (h + 1) * HD], gap]
    query = jnp.concatenate(spread, axis=1).astype(BF16)
    q_all[kv] = query

    pl.semaphore_wait(barrier, sources - 1 + tps - 1)

    q_sends = []
    for step in range(1, kvs):
        copy = pltpu.make_async_remote_copy(
            src_ref=q_all.at[kv],
            dst_ref=q_all.at[kv],
            send_sem=q_send_sem.at[step],
            recv_sem=q_recv_sem.at[kv],
            device_id={"kv": lax.rem(kv + step, kvs)},
            device_id_type=MESH,
        )
        copy.start()
        q_sends.append(copy)
    for copy in small_loads[2:] + pair_loads + [out_load, up_load, down_load]:
        copy.start()

    lane = lax.broadcasted_iota(jnp.int32, (1, width), 1)
    lane_head = sum((lane >= h * PAIR).astype(jnp.int32) for h in range(1, heads))
    is_value = (lane - lane_head * PAIR) >= HD
    small_lane = lax.broadcasted_iota(jnp.int32, (1, 128), 1)
    for copy in small_loads[2:]:
        copy.wait()
    for step in range(1, kvs):
        other = lax.rem(kv + step, kvs)
        pltpu.make_async_remote_copy(
            src_ref=q_all.at[other],
            dst_ref=q_all.at[other],
            send_sem=q_send_sem.at[step],
            recv_sem=q_recv_sem.at[other],
            device_id={"kv": other},
            device_id_type=MESH,
        ).wait_recv()
    q_rows[...] = q_all[...].astype(F32).reshape(requests, width)

    head_row = lax.broadcasted_iota(jnp.int32, (8, 1), 0)
    key_mask = (lane_head == head_row) & ~is_value
    value_mask = (lane_head == head_row) & is_value
    token_lane = lax.broadcasted_iota(jnp.int32, (1, tokens), 1)

    owners, limits, scores, peaks = [], [], [], []
    for b in range(blocks):
        owner = owner_ref[0, b]
        clipped = jnp.minimum(owner, requests - 1)
        limit = jnp.where(
            owner < requests, length_ref[clipped] - index_ref[0, b] * tokens, 0
        )
        if b in (0, middle):
            cache_loads[b // middle].wait()
        q_row = q_rows[pl.ds(clipped, 1), :]
        block_query = jnp.where(key_mask, q_row, 0.0).astype(BF16)
        score = dot_last(block_query, cache[b])
        score = jnp.where(token_lane < limit, score, very_low)
        owners.append(owner)
        limits.append(limit)
        scores.append(score)
        peaks.append(jnp.max(score, axis=1, keepdims=True))

    slot_row = lax.broadcasted_iota(jnp.int32, (requests, 1), 0)
    sums = jnp.zeros((requests, width), F32)
    stats = jnp.where(small_lane < 8, very_low, 0.0) + jnp.zeros((requests, 128), F32)
    for b in range(blocks):
        shift = peaks[b]
        for other in range(blocks):
            if other != b:
                shift = jnp.where(
                    owners[other] == owners[b], jnp.maximum(shift, peaks[other]), shift
                )
        weight = jnp.where(token_lane < limits[b], jnp.exp(scores[b] - shift), 0.0)
        total = jnp.sum(weight, axis=1, keepdims=True)
        acc = dot_plain(weight.astype(BF16), cache[b])
        acc_row = jnp.sum(jnp.where(value_mask, acc, 0.0), axis=0, keepdims=True)
        stat_row = jnp.sum(
            jnp.where(
                small_lane == head_row, shift, jnp.where(small_lane == head_row + 8, total, 0.0)
            ),
            axis=0,
            keepdims=True,
        )
        mine = slot_row == owners[b]
        sums = sums + jnp.where(mine, acc_row, 0.0)
        stats = jnp.where(
            mine, jnp.where(small_lane < 8, stat_row, stats + stat_row), stats
        )
    stat_send[...] = stats.reshape(kvs, rows, 128)
    sums_send[...] = sums.reshape(kvs, rows, width).astype(BF16)

    partial_sends = []
    for step in range(1, sources):
        to = lax.rem(me + step, sources)
        to_kv = lax.rem(to, kvs)
        for src, dst, send_sem, recv_sem in (
            (stat_send, stat_recv, stat_send_sem, stat_recv_sem),
            (sums_send, sums_recv, sums_send_sem, sums_recv_sem),
        ):
            copy = pltpu.make_async_remote_copy(
                src_ref=src.at[to_kv],
                dst_ref=dst.at[me],
                send_sem=send_sem.at[step],
                recv_sem=recv_sem.at[me],
                device_id=source_id(to),
                device_id_type=MESH,
            )
            copy.start()
            partial_sends.append(copy)
    stat_recv[me] = stat_send[kv]
    sums_recv[me] = sums_send[kv]

    for copy in pair_loads:
        copy.wait()
    pairs = dot_last(normed, w_pair[...])
    fresh = pairs.astype(BF16).astype(F32)
    self_products = jnp.where(is_value, 0.0, query.astype(F32) * fresh)
    self_score = jnp.full((rows, 128), very_low, F32)
    for h in range(heads):
        score = jnp.sum(jnp.where(lane_head == h, self_products, 0.0), axis=1, keepdims=True)
        self_score = jnp.where(small_lane == h, score, self_score)
    fresh_values = jnp.where(is_value, fresh, 0.0)

    row_number = lax.broadcasted_iota(jnp.int32, (rows, 1), 0)
    target = jnp.zeros((rows, 1), jnp.int32)
    for i in range(rows):
        slot = kv * rows + i
        aim = jnp.bitwise_xor(home_ref[slot], moving_ref[slot])
        target = jnp.where(row_number == i, aim, target)
    served_here = target == rep
    entries_ref[0] = jnp.where(served_here, pairs, 0.0)

    for step in range(1, sources):
        other = lax.rem(me + step, sources)
        for dst, send_sem, recv_sem in (
            (stat_recv, stat_send_sem, stat_recv_sem),
            (sums_recv, sums_send_sem, sums_recv_sem),
        ):
            pltpu.make_async_remote_copy(
                src_ref=dst.at[other],
                dst_ref=dst.at[other],
                send_sem=send_sem.at[step],
                recv_sem=recv_sem.at[other],
                device_id=source_id(other),
                device_id_type=MESH,
            ).wait_recv()

    def over_lanes(values):
        wide = jnp.broadcast_to(values[:, heads - 1 : heads], (rows, width))
        for h in reversed(range(heads - 1)):
            wide = jnp.where(lane < (h + 1) * PAIR, values[:, h : h + 1], wide)
        return wide

    top = self_score
    for s in range(sources):
        top = jnp.maximum(top, stat_recv[s])
    in_heads = small_lane < heads
    self_weight = jnp.exp(self_score - top)
    denominator = self_weight
    factors = []
    for s in range(sources):
        stat = stat_recv[s]
        factor = jnp.exp(stat - top)
        factors.append(factor)
        denominator = denominator + pltpu.roll(stat, 120, 1) * factor
    share = 1.0 / jnp.where(in_heads, denominator, 1.0)
    attended = over_lanes(self_weight.astype(BF16).astype(F32) * share) * fresh_values
    for s in range(sources):
        attended = attended + over_lanes(factors[s] * share) * sums_recv[s].astype(F32)
    attended = jnp.concatenate(
        [attended[:, h * PAIR + HD : (h + 1) * PAIR] for h in range(heads)], axis=1
    ).astype(BF16)

    def summed_over_tp(part, buffer, send_sem, recv_sem):
        buffer[tp] = part.astype(BF16)
        sends = []
        for step in range(1, tps):
            copy = pltpu.make_async_remote_copy(
                src_ref=buffer.at[tp],
                dst_ref=buffer.at[tp],
                send_sem=send_sem.at[step],
                recv_sem=recv_sem.at[tp],
                device_id={"tp": lax.rem(tp + step, tps)},
                device_id_type=MESH,
            )
            copy.start()
            sends.append(copy)
        for step in range(1, tps):
            other = lax.rem(tp + step, tps)
            pltpu.make_async_remote_copy(
                src_ref=buffer.at[other],
                dst_ref=buffer.at[other],
                send_sem=send_sem.at[step],
                recv_sem=recv_sem.at[other],
                device_id={"tp": other},
                device_id_type=MESH,
            ).wait_recv()
        total = buffer[0].astype(F32)
        for t in range(1, tps):
            total = total + buffer[t].astype(F32)
        return total, sends

    out_load.wait()
    attn_out, out_sends = summed_over_tp(
        dot_plain(attended, w_out[...]), part_out, out_send_sem, out_recv_sem
    )
    residual = state + attn_out
    normed_mlp = root_norm(residual, mlp_gain_ref[...].reshape(1, -1)).astype(BF16)
    up_load.wait()
    activated = gelu_tanh(dot_last(normed_mlp, w_up[...])).astype(BF16)
    down_load.wait()
    mlp_out, down_sends = summed_over_tp(
        dot_plain(activated, w_down[...]), part_down, down_send_sem, down_recv_sem
    )
    hidden_ref[0] = jnp.where(served_here, residual + mlp_out, 0.0)
    for copy in q_sends + partial_sends + out_sends + down_sends:
        copy.wait_send()


def body(
    reps,
    kvs,
    tps,
    token_state,
    attn_gain,
    qkv_weight,
    out_weight,
    mlp_gain,
    up_weight,
    down_weight,
    kv_cache,
    home_replica,
    moving,
    cache_length,
    block_owner,
    block_index,
):
    rows, model = token_state.shape
    requests = home_replica.shape[0]
    heads = out_weight.shape[0] // HD
    hidden_units = down_weight.shape[0]
    _, blocks, tokens, width = kv_cache.shape
    sources = reps * kvs
    sizes = (reps, kvs, tps, heads, blocks, tokens, rows, requests)
    vmem = pl.BlockSpec(memory_space=pltpu.VMEM)
    in_hbm = pl.BlockSpec(memory_space=pltpu.HBM)
    dma = pltpu.SemaphoreType.DMA
    return pl.pallas_call(
        functools.partial(kernel, sizes),
        out_shape=(
            pltpu.VMEM((1, rows, model), F32),
            pltpu.VMEM((1, rows, width), F32),
        ),
        in_specs=[in_hbm] * 13,
        out_specs=(vmem, vmem),
        scratch_shapes=[
            pltpu.VMEM((rows, model), BF16),
            pltpu.VMEM((model,), F32),
            pltpu.VMEM((model,), F32),
            pltpu.SMEM((requests,), jnp.int32),
            pltpu.SMEM((requests,), jnp.int32),
            pltpu.SMEM((requests,), jnp.int32),
            pltpu.SMEM((1, blocks), jnp.int32),
            pltpu.SMEM((1, blocks), jnp.int32),
            pltpu.VMEM((heads * HD, model), BF16),
            pltpu.VMEM((width, model), BF16),
            pltpu.VMEM((heads * HD, model), BF16),
            pltpu.VMEM((hidden_units, model), BF16),
            pltpu.VMEM((hidden_units, model), BF16),
            pltpu.VMEM((blocks, tokens, width), BF16),
            pltpu.VMEM((kvs, rows, width), BF16),
            pltpu.VMEM((requests, width), F32),
            pltpu.VMEM((kvs, rows, 128), F32),
            pltpu.VMEM((kvs, rows, width), BF16),
            pltpu.VMEM((sources, rows, 128), F32),
            pltpu.VMEM((sources, rows, width), BF16),
            pltpu.VMEM((tps, rows, model), BF16),
            pltpu.VMEM((tps, rows, model), BF16),
            dma((8,)),
            dma((2 * heads + 3,)),
            dma((2,)),
            dma((kvs,)),
            dma((kvs,)),
            dma((sources,)),
            dma((sources,)),
            dma((sources,)),
            dma((sources,)),
            dma((tps,)),
            dma((tps,)),
            dma((tps,)),
            dma((tps,)),
        ],
        compiler_params=pltpu.CompilerParams(
            collective_id=0, has_side_effects=True, vmem_limit_bytes=56 * 1024 * 1024
        ),
        name="decode_layer",
    )(
        token_state,
        attn_gain,
        mlp_gain,
        home_replica,
        moving,
        cache_length,
        block_owner,
        block_index,
        qkv_weight.T,
        out_weight,
        up_weight.T,
        down_weight,
        kv_cache,
    )


def solution(mesh):
    return jax.shard_map(
        functools.partial(body, mesh.shape["rep"], mesh.shape["kv"], mesh.shape["tp"]),
        mesh=mesh,
        in_specs=(
            P("kv", None),
            P(),
            P(None, "tp"),
            P("tp", None),
            P(),
            P(None, "tp"),
            P("tp", None),
            P("rep", "kv", None, "tp"),
            P(),
            P(),
            P(),
            P("rep", "kv"),
            P("rep", "kv"),
        ),
        out_specs=(P("rep", "kv", None), P("rep", "kv", "tp")),
        check_vma=False,
    )
```

```python
import functools

import jax
import jax.numpy as jnp
from jax import lax
from jax.experimental import pallas as pl
from jax.experimental.pallas import tpu as pltpu
from jax.sharding import PartitionSpec as P

HD = 80
PAIR = 2 * HD

very_low = -1e30
norm_eps = 1e-06

MESH = pl.DeviceIdType.MESH
BF16 = jnp.bfloat16
F32 = jnp.float32


def root_norm(values_in, gain_vector):
    values_in = values_in.astype(F32)
    scaled = values_in * lax.rsqrt(
        jnp.mean(values_in * values_in, axis=-1, keepdims=True) + norm_eps
    )
    return scaled * gain_vector


def gelu_tanh(x):
    return 0.5 * x * (1.0 + jnp.tanh(0.7978845608028654 * (x + 0.044715 * (x * x * x))))


def dot_last(left, right):
    return lax.dot_general(left, right, (((1,), (1,)), ((), ())), preferred_element_type=F32)


def dot_plain(left, right):
    return lax.dot_general(left, right, (((1,), (0,)), ((), ())), preferred_element_type=F32)


def kernel(
    sizes,
    state_hbm,
    attn_gain_hbm,
    mlp_gain_hbm,
    home_hbm,
    moving_hbm,
    length_hbm,
    owner_hbm,
    index_hbm,
    qkv_hbm,
    out_hbm,
    up_hbm,
    down_hbm,
    cache_hbm,
    hidden_ref,
    entries_ref,
    state_ref,
    attn_gain_ref,
    mlp_gain_ref,
    home_ref,
    moving_ref,
    length_ref,
    owner_ref,
    index_ref,
    w_query,
    w_pair,
    w_out,
    w_up,
    w_down,
    cache,
    q_all,
    q_rows,
    stat_send,
    sums_send,
    stat_recv,
    sums_recv,
    part_out,
    part_down,
    small_sem,
    load_sem,
    cache_sem,
    q_send_sem,
    q_recv_sem,
    stat_send_sem,
    stat_recv_sem,
    sums_send_sem,
    sums_recv_sem,
    out_send_sem,
    out_recv_sem,
    down_send_sem,
    down_recv_sem,
):
    reps, kvs, tps, heads, blocks, tokens, rows, requests = sizes
    width = heads * PAIR
    sources = reps * kvs
    rep = lax.axis_index("rep")
    kv = lax.axis_index("kv")
    tp = lax.axis_index("tp")
    me = rep * kvs + kv

    def source_id(number):
        return {"rep": lax.div(number, kvs), "kv": lax.rem(number, kvs)}

    barrier = pltpu.get_barrier_semaphore()
    for step in range(1, sources):
        pl.semaphore_signal(
            barrier,
            inc=1,
            device_id=source_id(lax.rem(me + step, sources)),
            device_id_type=MESH,
        )
    for step in range(1, tps):
        pl.semaphore_signal(
            barrier, inc=1, device_id={"tp": lax.rem(tp + step, tps)}, device_id_type=MESH
        )

    small_loads = [
        pltpu.make_async_copy(source, held, small_sem.at[i])
        for i, (source, held) in enumerate(
            (
                (state_hbm, state_ref),
                (attn_gain_hbm, attn_gain_ref),
                (mlp_gain_hbm, mlp_gain_ref),
                (home_hbm, home_ref),
                (moving_hbm, moving_ref),
                (length_hbm, length_ref),
                (owner_hbm, owner_ref),
                (index_hbm, index_ref),
            )
        )
    ]
    query_loads, pair_loads = [], []
    for h in range(heads):
        query_loads.append(
            pltpu.make_async_copy(
                qkv_hbm.at[pl.ds(h * 3 * HD, HD)],
                w_query.at[pl.ds(h * HD, HD)],
                load_sem.at[h],
            )
        )
        pair_loads.append(
            pltpu.make_async_copy(
                qkv_hbm.at[pl.ds(h * 3 * HD + HD, PAIR)],
                w_pair.at[pl.ds(h * PAIR, PAIR)],
                load_sem.at[heads + h],
            )
        )
    out_load = pltpu.make_async_copy(out_hbm, w_out, load_sem.at[2 * heads])
    up_load = pltpu.make_async_copy(up_hbm, w_up, load_sem.at[2 * heads + 1])
    down_load = pltpu.make_async_copy(down_hbm, w_down, load_sem.at[2 * heads + 2])
    cache_loads = [
        pltpu.make_async_copy(cache_hbm.at[0, b], cache.at[b], cache_sem.at[b])
        for b in range(blocks)
    ]
    for copy in small_loads[:2] + query_loads + small_loads[2:] + cache_loads:
        copy.start()
    for copy in pair_loads + [out_load, up_load, down_load]:
        copy.start()
    for copy in small_loads[:2]:
        copy.wait()

    state = state_ref[...].astype(F32)
    normed = root_norm(state, attn_gain_ref[...].reshape(1, -1)).astype(BF16)
    for copy in query_loads:
        copy.wait()
    compact = dot_last(normed, w_query[...]) * HD ** (-0.5)
    gap = jnp.zeros((rows, HD), F32)
    spread = []
    for h in range(heads):
        spread += [compact[:, h * HD : (h + 1) * HD], gap]
    query = jnp.concatenate(spread, axis=1).astype(BF16)
    q_all[kv] = query

    pl.semaphore_wait(barrier, sources - 1 + tps - 1)

    q_sends = []
    for step in range(1, kvs):
        copy = pltpu.make_async_remote_copy(
            src_ref=q_all.at[kv],
            dst_ref=q_all.at[kv],
            send_sem=q_send_sem.at[step],
            recv_sem=q_recv_sem.at[kv],
            device_id={"kv": lax.rem(kv + step, kvs)},
            device_id_type=MESH,
        )
        copy.start()
        q_sends.append(copy)

    lane = lax.broadcasted_iota(jnp.int32, (1, width), 1)
    lane_head = sum((lane >= h * PAIR).astype(jnp.int32) for h in range(1, heads))
    is_value = (lane - lane_head * PAIR) >= HD
    small_lane = lax.broadcasted_iota(jnp.int32, (1, 128), 1)
    for copy in small_loads[2:]:
        copy.wait()
    for step in range(1, kvs):
        other = lax.rem(kv + step, kvs)
        pltpu.make_async_remote_copy(
            src_ref=q_all.at[other],
            dst_ref=q_all.at[other],
            send_sem=q_send_sem.at[step],
            recv_sem=q_recv_sem.at[other],
            device_id={"kv": other},
            device_id_type=MESH,
        ).wait_recv()
    q_rows[...] = q_all[...].astype(F32).reshape(requests, width)

    head_row = lax.broadcasted_iota(jnp.int32, (8, 1), 0)
    key_mask = (lane_head == head_row) & ~is_value
    value_mask = (lane_head == head_row) & is_value
    token_lane = lax.broadcasted_iota(jnp.int32, (1, tokens), 1)

    for copy in cache_loads:
        copy.wait()
    owners, limits, scores, peaks = [], [], [], []
    for b in range(blocks):
        owner = owner_ref[0, b]
        clipped = jnp.minimum(owner, requests - 1)
        limit = jnp.where(
            owner < requests, length_ref[clipped] - index_ref[0, b] * tokens, 0
        )
        q_row = q_rows[pl.ds(clipped, 1), :]
        block_query = jnp.where(key_mask, q_row, 0.0).astype(BF16)
        score = dot_last(block_query, cache[b])
        score = jnp.where(token_lane < limit, score, very_low)
        owners.append(owner)
        limits.append(limit)
        scores.append(score)
        peaks.append(jnp.max(score, axis=1, keepdims=True))

    def values_only(wide):
        return jnp.concatenate(
            [wide[:, h * PAIR + HD : (h + 1) * PAIR] for h in range(heads)], axis=1
        )

    slot_row = lax.broadcasted_iota(jnp.int32, (requests, 1), 0)
    sums = jnp.zeros((requests, width), F32)
    stats = jnp.where(small_lane < 8, very_low, 0.0) + jnp.zeros((requests, 128), F32)
    for b in range(blocks):
        shift = peaks[b]
        for other in range(blocks):
            if other != b:
                shift = jnp.where(
                    owners[other] == owners[b], jnp.maximum(shift, peaks[other]), shift
                )
        weight = jnp.where(token_lane < limits[b], jnp.exp(scores[b] - shift), 0.0)
        total = jnp.sum(weight, axis=1, keepdims=True)
        acc = dot_plain(weight.astype(BF16), cache[b])
        acc_row = jnp.sum(jnp.where(value_mask, acc, 0.0), axis=0, keepdims=True)
        stat_row = jnp.sum(
            jnp.where(
                small_lane == head_row, shift, jnp.where(small_lane == head_row + 8, total, 0.0)
            ),
            axis=0,
            keepdims=True,
        )
        mine = slot_row == owners[b]
        sums = sums + jnp.where(mine, acc_row, 0.0)
        stats = jnp.where(
            mine, jnp.where(small_lane < 8, stat_row, stats + stat_row), stats
        )
    stat_send[...] = stats.reshape(kvs, rows, 128)
    sums_send[...] = values_only(sums).reshape(kvs, rows, heads * HD).astype(BF16)

    partial_sends = []
    for step in range(1, sources):
        to = lax.rem(me + step, sources)
        to_kv = lax.rem(to, kvs)
        for src, dst, send_sem, recv_sem in (
            (stat_send, stat_recv, stat_send_sem, stat_recv_sem),
            (sums_send, sums_recv, sums_send_sem, sums_recv_sem),
        ):
            copy = pltpu.make_async_remote_copy(
                src_ref=src.at[to_kv],
                dst_ref=dst.at[me],
                send_sem=send_sem.at[step],
                recv_sem=recv_sem.at[me],
                device_id=source_id(to),
                device_id_type=MESH,
            )
            copy.start()
            partial_sends.append(copy)
    stat_recv[me] = stat_send[kv]
    sums_recv[me] = sums_send[kv]

    for copy in pair_loads:
        copy.wait()
    pairs = dot_last(normed, w_pair[...])
    fresh = pairs.astype(BF16).astype(F32)
    self_products = jnp.where(is_value, 0.0, query.astype(F32) * fresh)
    self_score = jnp.full((rows, 128), very_low, F32)
    for h in range(heads):
        score = jnp.sum(jnp.where(lane_head == h, self_products, 0.0), axis=1, keepdims=True)
        self_score = jnp.where(small_lane == h, score, self_score)
    fresh_values = values_only(fresh)

    row_number = lax.broadcasted_iota(jnp.int32, (rows, 1), 0)
    target = jnp.zeros((rows, 1), jnp.int32)
    for i in range(rows):
        slot = kv * rows + i
        aim = jnp.bitwise_xor(home_ref[slot], moving_ref[slot])
        target = jnp.where(row_number == i, aim, target)
    served_here = target == rep
    entries_ref[0] = jnp.where(served_here, pairs, 0.0)

    for step in range(1, sources):
        other = lax.rem(me + step, sources)
        for dst, send_sem, recv_sem in (
            (stat_recv, stat_send_sem, stat_recv_sem),
            (sums_recv, sums_send_sem, sums_recv_sem),
        ):
            pltpu.make_async_remote_copy(
                src_ref=dst.at[other],
                dst_ref=dst.at[other],
                send_sem=send_sem.at[step],
                recv_sem=recv_sem.at[other],
                device_id=source_id(other),
                device_id_type=MESH,
            ).wait_recv()

    value_lane = lax.broadcasted_iota(jnp.int32, (1, heads * HD), 1)

    def over_lanes(values):
        wide = jnp.broadcast_to(values[:, heads - 1 : heads], (rows, heads * HD))
        for h in reversed(range(heads - 1)):
            wide = jnp.where(value_lane < (h + 1) * HD, values[:, h : h + 1], wide)
        return wide

    top = self_score
    for s in range(sources):
        top = jnp.maximum(top, stat_recv[s])
    in_heads = small_lane < heads
    self_weight = jnp.exp(self_score - top)
    denominator = self_weight
    factors = []
    for s in range(sources):
        stat = stat_recv[s]
        factor = jnp.exp(stat - top)
        factors.append(factor)
        denominator = denominator + pltpu.roll(stat, 120, 1) * factor
    share = 1.0 / jnp.where(in_heads, denominator, 1.0)
    attended = over_lanes(self_weight.astype(BF16).astype(F32) * share) * fresh_values
    for s in range(sources):
        attended = attended + over_lanes(factors[s] * share) * sums_recv[s].astype(F32)
    attended = attended.astype(BF16)

    def summed_over_tp(part, buffer, send_sem, recv_sem):
        buffer[tp] = part.astype(BF16)
        sends = []
        for step in range(1, tps):
            copy = pltpu.make_async_remote_copy(
                src_ref=buffer.at[tp],
                dst_ref=buffer.at[tp],
                send_sem=send_sem.at[step],
                recv_sem=recv_sem.at[tp],
                device_id={"tp": lax.rem(tp + step, tps)},
                device_id_type=MESH,
            )
            copy.start()
            sends.append(copy)
        for step in range(1, tps):
            other = lax.rem(tp + step, tps)
            pltpu.make_async_remote_copy(
                src_ref=buffer.at[other],
                dst_ref=buffer.at[other],
                send_sem=send_sem.at[step],
                recv_sem=recv_sem.at[other],
                device_id={"tp": other},
                device_id_type=MESH,
            ).wait_recv()
        total = buffer[0].astype(F32)
        for t in range(1, tps):
            total = total + buffer[t].astype(F32)
        return total, sends

    out_load.wait()
    attn_out, out_sends = summed_over_tp(
        dot_plain(attended, w_out[...]), part_out, out_send_sem, out_recv_sem
    )
    residual = state + attn_out
    normed_mlp = root_norm(residual, mlp_gain_ref[...].reshape(1, -1)).astype(BF16)
    up_load.wait()
    activated = gelu_tanh(dot_last(normed_mlp, w_up[...])).astype(BF16)
    down_load.wait()
    mlp_out, down_sends = summed_over_tp(
        dot_plain(activated, w_down[...]), part_down, down_send_sem, down_recv_sem
    )
    hidden_ref[0] = jnp.where(served_here, residual + mlp_out, 0.0)
    for copy in q_sends + partial_sends + out_sends + down_sends:
        copy.wait_send()


def body(
    reps,
    kvs,
    tps,
    token_state,
    attn_gain,
    qkv_weight,
    out_weight,
    mlp_gain,
    up_weight,
    down_weight,
    kv_cache,
    home_replica,
    moving,
    cache_length,
    block_owner,
    block_index,
):
    rows, model = token_state.shape
    requests = home_replica.shape[0]
    heads = out_weight.shape[0] // HD
    hidden_units = down_weight.shape[0]
    _, blocks, tokens, width = kv_cache.shape
    sources = reps * kvs
    sizes = (reps, kvs, tps, heads, blocks, tokens, rows, requests)
    vmem = pl.BlockSpec(memory_space=pltpu.VMEM)
    in_hbm = pl.BlockSpec(memory_space=pltpu.HBM)
    dma = pltpu.SemaphoreType.DMA
    return pl.pallas_call(
        functools.partial(kernel, sizes),
        out_shape=(
            pltpu.VMEM((1, rows, model), F32),
            pltpu.VMEM((1, rows, width), F32),
        ),
        in_specs=[in_hbm] * 13,
        out_specs=(vmem, vmem),
        scratch_shapes=[
            pltpu.VMEM((rows, model), BF16),
            pltpu.VMEM((model,), F32),
            pltpu.VMEM((model,), F32),
            pltpu.SMEM((requests,), jnp.int32),
            pltpu.SMEM((requests,), jnp.int32),
            pltpu.SMEM((requests,), jnp.int32),
            pltpu.SMEM((1, blocks), jnp.int32),
            pltpu.SMEM((1, blocks), jnp.int32),
            pltpu.VMEM((heads * HD, model), BF16),
            pltpu.VMEM((width, model), BF16),
            pltpu.VMEM((heads * HD, model), BF16),
            pltpu.VMEM((hidden_units, model), BF16),
            pltpu.VMEM((hidden_units, model), BF16),
            pltpu.VMEM((blocks, tokens, width), BF16),
            pltpu.VMEM((kvs, rows, width), BF16),
            pltpu.VMEM((requests, width), F32),
            pltpu.VMEM((kvs, rows, 128), F32),
            pltpu.VMEM((kvs, rows, heads * HD), BF16),
            pltpu.VMEM((sources, rows, 128), F32),
            pltpu.VMEM((sources, rows, heads * HD), BF16),
            pltpu.VMEM((tps, rows, model), BF16),
            pltpu.VMEM((tps, rows, model), BF16),
            dma((8,)),
            dma((2 * heads + 3,)),
            dma((blocks,)),
            dma((kvs,)),
            dma((kvs,)),
            dma((sources,)),
            dma((sources,)),
            dma((sources,)),
            dma((sources,)),
            dma((tps,)),
            dma((tps,)),
            dma((tps,)),
            dma((tps,)),
        ],
        compiler_params=pltpu.CompilerParams(
            collective_id=0, has_side_effects=True, vmem_limit_bytes=56 * 1024 * 1024
        ),
        name="decode_layer",
    )(
        token_state,
        attn_gain,
        mlp_gain,
        home_replica,
        moving,
        cache_length,
        block_owner,
        block_index,
        qkv_weight.T,
        out_weight,
        up_weight.T,
        down_weight,
        kv_cache,
    )


def solution(mesh):
    return jax.shard_map(
        functools.partial(body, mesh.shape["rep"], mesh.shape["kv"], mesh.shape["tp"]),
        mesh=mesh,
        in_specs=(
            P("kv", None),
            P(),
            P(None, "tp"),
            P("tp", None),
            P(),
            P(None, "tp"),
            P("tp", None),
            P("rep", "kv", None, "tp"),
            P(),
            P(),
            P(),
            P("rep", "kv"),
            P("rep", "kv"),
        ),
        out_specs=(P("rep", "kv", None), P("rep", "kv", "tp")),
        check_vma=False,
    )
```

```python
import functools

import jax
import jax.numpy as jnp
from jax import lax
from jax.experimental import pallas as pl
from jax.experimental.pallas import tpu as pltpu
from jax.sharding import PartitionSpec as P

HD = 80
PAIR = 2 * HD

very_low = -1e30
norm_eps = 1e-06

MESH = pl.DeviceIdType.MESH
BF16 = jnp.bfloat16
F32 = jnp.float32


def root_norm(values_in, gain_vector):
    values_in = values_in.astype(F32)
    scaled = values_in * lax.rsqrt(
        jnp.mean(values_in * values_in, axis=-1, keepdims=True) + norm_eps
    )
    return scaled * gain_vector


def gelu_tanh(x):
    return 0.5 * x * (1.0 + jnp.tanh(0.7978845608028654 * (x + 0.044715 * (x * x * x))))


def dot_last(left, right):
    return lax.dot_general(left, right, (((1,), (1,)), ((), ())), preferred_element_type=F32)


def dot_plain(left, right):
    return lax.dot_general(left, right, (((1,), (0,)), ((), ())), preferred_element_type=F32)


def kernel(
    sizes,
    state_hbm,
    attn_gain_hbm,
    mlp_gain_hbm,
    home_hbm,
    moving_hbm,
    length_hbm,
    owner_hbm,
    index_hbm,
    qkv_hbm,
    out_hbm,
    up_hbm,
    down_hbm,
    cache_hbm,
    hidden_ref,
    entries_ref,
    state_ref,
    attn_gain_ref,
    mlp_gain_ref,
    home_ref,
    moving_ref,
    length_ref,
    owner_ref,
    index_ref,
    w_query,
    w_pair,
    w_out,
    w_up,
    w_down,
    cache,
    q_all,
    q_rows,
    stat_send,
    sums_send,
    stat_recv,
    sums_recv,
    part_out,
    part_down,
    small_sem,
    load_sem,
    cache_sem,
    q_send_sem,
    q_recv_sem,
    stat_send_sem,
    stat_recv_sem,
    sums_send_sem,
    sums_recv_sem,
    out_send_sem,
    out_recv_sem,
    down_send_sem,
    down_recv_sem,
):
    reps, kvs, tps, heads, blocks, tokens, rows, requests = sizes
    width = heads * PAIR
    sources = reps * kvs
    rep = lax.axis_index("rep")
    kv = lax.axis_index("kv")
    tp = lax.axis_index("tp")
    me = rep * kvs + kv

    def source_id(number):
        return {"rep": lax.div(number, kvs), "kv": lax.rem(number, kvs)}

    barrier = pltpu.get_barrier_semaphore()
    for step in range(1, sources):
        pl.semaphore_signal(
            barrier,
            inc=1,
            device_id=source_id(lax.rem(me + step, sources)),
            device_id_type=MESH,
        )
    for step in range(1, tps):
        pl.semaphore_signal(
            barrier, inc=1, device_id={"tp": lax.rem(tp + step, tps)}, device_id_type=MESH
        )

    small_loads = [
        pltpu.make_async_copy(source, held, small_sem.at[i])
        for i, (source, held) in enumerate(
            (
                (state_hbm, state_ref),
                (attn_gain_hbm, attn_gain_ref),
                (mlp_gain_hbm, mlp_gain_ref),
                (home_hbm, home_ref),
                (moving_hbm, moving_ref),
                (length_hbm, length_ref),
                (owner_hbm, owner_ref),
                (index_hbm, index_ref),
            )
        )
    ]
    query_loads, pair_loads = [], []
    for h in range(heads):
        query_loads.append(
            pltpu.make_async_copy(
                qkv_hbm.at[pl.ds(h * 3 * HD, HD)],
                w_query.at[pl.ds(h * HD, HD)],
                load_sem.at[h],
            )
        )
        pair_loads.append(
            pltpu.make_async_copy(
                qkv_hbm.at[pl.ds(h * 3 * HD + HD, PAIR)],
                w_pair.at[pl.ds(h * PAIR, PAIR)],
                load_sem.at[heads + h],
            )
        )
    out_load = pltpu.make_async_copy(out_hbm, w_out, load_sem.at[2 * heads])
    up_load = pltpu.make_async_copy(up_hbm, w_up, load_sem.at[2 * heads + 1])
    down_load = pltpu.make_async_copy(down_hbm, w_down, load_sem.at[2 * heads + 2])
    cache_loads = [
        pltpu.make_async_copy(cache_hbm.at[0, b], cache.at[b], cache_sem.at[b])
        for b in range(blocks)
    ]
    for copy in small_loads[:2] + query_loads + small_loads[2:] + cache_loads:
        copy.start()
    for copy in pair_loads + [out_load, up_load, down_load]:
        copy.start()
    for copy in small_loads[:2]:
        copy.wait()

    state = state_ref[...].astype(F32)
    normed = root_norm(state, attn_gain_ref[...].reshape(1, -1)).astype(BF16)
    for copy in query_loads:
        copy.wait()
    compact = dot_last(normed, w_query[...]) * HD ** (-0.5)
    gap = jnp.zeros((rows, HD), F32)
    spread = []
    for h in range(heads):
        spread += [compact[:, h * HD : (h + 1) * HD], gap]
    query = jnp.concatenate(spread, axis=1).astype(BF16)
    q_all[kv] = query

    pl.semaphore_wait(barrier, sources - 1 + tps - 1)

    q_sends = []
    for step in range(1, kvs):
        copy = pltpu.make_async_remote_copy(
            src_ref=q_all.at[kv],
            dst_ref=q_all.at[kv],
            send_sem=q_send_sem.at[step],
            recv_sem=q_recv_sem.at[kv],
            device_id={"kv": lax.rem(kv + step, kvs)},
            device_id_type=MESH,
        )
        copy.start()
        q_sends.append(copy)

    lane = lax.broadcasted_iota(jnp.int32, (1, width), 1)
    lane_head = sum((lane >= h * PAIR).astype(jnp.int32) for h in range(1, heads))
    is_value = (lane - lane_head * PAIR) >= HD
    small_lane = lax.broadcasted_iota(jnp.int32, (1, 128), 1)
    for copy in small_loads[2:]:
        copy.wait()
    for step in range(1, kvs):
        other = lax.rem(kv + step, kvs)
        pltpu.make_async_remote_copy(
            src_ref=q_all.at[other],
            dst_ref=q_all.at[other],
            send_sem=q_send_sem.at[step],
            recv_sem=q_recv_sem.at[other],
            device_id={"kv": other},
            device_id_type=MESH,
        ).wait_recv()
    q_rows[...] = q_all[...].astype(F32).reshape(requests, width)

    head_row = lax.broadcasted_iota(jnp.int32, (8, 1), 0)
    key_mask = (lane_head == head_row) & ~is_value
    value_mask = (lane_head == head_row) & is_value
    token_lane = lax.broadcasted_iota(jnp.int32, (1, tokens), 1)

    for copy in cache_loads:
        copy.wait()
    owners, peaks, totals, accs = [], [], [], []
    for b in range(blocks):
        owner = owner_ref[0, b]
        clipped = jnp.minimum(owner, requests - 1)
        limit = jnp.where(
            owner < requests, length_ref[clipped] - index_ref[0, b] * tokens, 0
        )
        q_row = q_rows[pl.ds(clipped, 1), :]
        block_query = jnp.where(key_mask, q_row, 0.0).astype(BF16)
        score = dot_last(block_query, cache[b])
        usable = token_lane < limit
        score = jnp.where(usable, score, very_low)
        peak = jnp.max(score, axis=1, keepdims=True)
        weight = jnp.where(usable, jnp.exp(score - peak), 0.0)
        owners.append(owner)
        peaks.append(peak)
        totals.append(jnp.sum(weight, axis=1, keepdims=True))
        accs.append(dot_plain(weight.astype(BF16), cache[b]))

    def values_only(wide):
        return jnp.concatenate(
            [wide[:, h * PAIR + HD : (h + 1) * PAIR] for h in range(heads)], axis=1
        )

    slot_row = lax.broadcasted_iota(jnp.int32, (requests, 1), 0)
    sums = jnp.zeros((requests, width), F32)
    stats = jnp.where(small_lane < 8, very_low, 0.0) + jnp.zeros((requests, 128), F32)
    for b in range(blocks):
        shift = peaks[b]
        for other in range(blocks):
            if other != b:
                shift = jnp.where(
                    owners[other] == owners[b], jnp.maximum(shift, peaks[other]), shift
                )
        scale = jnp.exp(peaks[b] - shift)
        total = totals[b] * scale
        acc_row = jnp.sum(jnp.where(value_mask, accs[b] * scale, 0.0), axis=0, keepdims=True)
        stat_row = jnp.sum(
            jnp.where(
                small_lane == head_row, shift, jnp.where(small_lane == head_row + 8, total, 0.0)
            ),
            axis=0,
            keepdims=True,
        )
        mine = slot_row == owners[b]
        sums = sums + jnp.where(mine, acc_row, 0.0)
        stats = jnp.where(
            mine, jnp.where(small_lane < 8, stat_row, stats + stat_row), stats
        )
    stat_send[...] = stats.reshape(kvs, rows, 128)
    sums_send[...] = values_only(sums).reshape(kvs, rows, heads * HD).astype(BF16)

    partial_sends = []
    for step in range(1, sources):
        to = lax.rem(me + step, sources)
        to_kv = lax.rem(to, kvs)
        for src, dst, send_sem, recv_sem in (
            (stat_send, stat_recv, stat_send_sem, stat_recv_sem),
            (sums_send, sums_recv, sums_send_sem, sums_recv_sem),
        ):
            copy = pltpu.make_async_remote_copy(
                src_ref=src.at[to_kv],
                dst_ref=dst.at[me],
                send_sem=send_sem.at[step],
                recv_sem=recv_sem.at[me],
                device_id=source_id(to),
                device_id_type=MESH,
            )
            copy.start()
            partial_sends.append(copy)
    stat_recv[me] = stat_send[kv]
    sums_recv[me] = sums_send[kv]

    for copy in pair_loads:
        copy.wait()
    pairs = dot_last(normed, w_pair[...])
    fresh = pairs.astype(BF16).astype(F32)
    self_products = jnp.where(is_value, 0.0, query.astype(F32) * fresh)
    self_score = jnp.full((rows, 128), very_low, F32)
    for h in range(heads):
        score = jnp.sum(jnp.where(lane_head == h, self_products, 0.0), axis=1, keepdims=True)
        self_score = jnp.where(small_lane == h, score, self_score)
    fresh_values = values_only(fresh)

    row_number = lax.broadcasted_iota(jnp.int32, (rows, 1), 0)
    target = jnp.zeros((rows, 1), jnp.int32)
    for i in range(rows):
        slot = kv * rows + i
        aim = jnp.bitwise_xor(home_ref[slot], moving_ref[slot])
        target = jnp.where(row_number == i, aim, target)
    served_here = target == rep
    entries_ref[0] = jnp.where(served_here, pairs, 0.0)

    for step in range(1, sources):
        other = lax.rem(me + step, sources)
        for dst, send_sem, recv_sem in (
            (stat_recv, stat_send_sem, stat_recv_sem),
            (sums_recv, sums_send_sem, sums_recv_sem),
        ):
            pltpu.make_async_remote_copy(
                src_ref=dst.at[other],
                dst_ref=dst.at[other],
                send_sem=send_sem.at[step],
                recv_sem=recv_sem.at[other],
                device_id=source_id(other),
                device_id_type=MESH,
            ).wait_recv()

    value_lane = lax.broadcasted_iota(jnp.int32, (1, heads * HD), 1)

    def over_lanes(values):
        wide = jnp.broadcast_to(values[:, heads - 1 : heads], (rows, heads * HD))
        for h in reversed(range(heads - 1)):
            wide = jnp.where(value_lane < (h + 1) * HD, values[:, h : h + 1], wide)
        return wide

    top = self_score
    for s in range(sources):
        top = jnp.maximum(top, stat_recv[s])
    in_heads = small_lane < heads
    self_weight = jnp.exp(self_score - top)
    denominator = self_weight
    factors = []
    for s in range(sources):
        stat = stat_recv[s]
        factor = jnp.exp(stat - top)
        factors.append(factor)
        denominator = denominator + pltpu.roll(stat, 120, 1) * factor
    share = 1.0 / jnp.where(in_heads, denominator, 1.0)
    attended = over_lanes(self_weight.astype(BF16).astype(F32) * share) * fresh_values
    for s in range(sources):
        attended = attended + over_lanes(factors[s] * share) * sums_recv[s].astype(F32)
    attended = attended.astype(BF16)

    def summed_over_tp(part, buffer, send_sem, recv_sem):
        buffer[tp] = part.astype(BF16)
        sends = []
        for step in range(1, tps):
            copy = pltpu.make_async_remote_copy(
                src_ref=buffer.at[tp],
                dst_ref=buffer.at[tp],
                send_sem=send_sem.at[step],
                recv_sem=recv_sem.at[tp],
                device_id={"tp": lax.rem(tp + step, tps)},
                device_id_type=MESH,
            )
            copy.start()
            sends.append(copy)
        for step in range(1, tps):
            other = lax.rem(tp + step, tps)
            pltpu.make_async_remote_copy(
                src_ref=buffer.at[other],
                dst_ref=buffer.at[other],
                send_sem=send_sem.at[step],
                recv_sem=recv_sem.at[other],
                device_id={"tp": other},
                device_id_type=MESH,
            ).wait_recv()
        total = buffer[0].astype(F32)
        for t in range(1, tps):
            total = total + buffer[t].astype(F32)
        return total, sends

    out_load.wait()
    attn_out, out_sends = summed_over_tp(
        dot_plain(attended, w_out[...]), part_out, out_send_sem, out_recv_sem
    )
    residual = state + attn_out
    normed_mlp = root_norm(residual, mlp_gain_ref[...].reshape(1, -1)).astype(BF16)
    up_load.wait()
    activated = gelu_tanh(dot_last(normed_mlp, w_up[...])).astype(BF16)
    down_load.wait()
    mlp_out, down_sends = summed_over_tp(
        dot_plain(activated, w_down[...]), part_down, down_send_sem, down_recv_sem
    )
    hidden_ref[0] = jnp.where(served_here, residual + mlp_out, 0.0)
    for copy in q_sends + partial_sends + out_sends + down_sends:
        copy.wait_send()


def body(
    reps,
    kvs,
    tps,
    token_state,
    attn_gain,
    qkv_weight,
    out_weight,
    mlp_gain,
    up_weight,
    down_weight,
    kv_cache,
    home_replica,
    moving,
    cache_length,
    block_owner,
    block_index,
):
    rows, model = token_state.shape
    requests = home_replica.shape[0]
    heads = out_weight.shape[0] // HD
    hidden_units = down_weight.shape[0]
    _, blocks, tokens, width = kv_cache.shape
    sources = reps * kvs
    sizes = (reps, kvs, tps, heads, blocks, tokens, rows, requests)
    vmem = pl.BlockSpec(memory_space=pltpu.VMEM)
    in_hbm = pl.BlockSpec(memory_space=pltpu.HBM)
    dma = pltpu.SemaphoreType.DMA
    return pl.pallas_call(
        functools.partial(kernel, sizes),
        out_shape=(
            pltpu.VMEM((1, rows, model), F32),
            pltpu.VMEM((1, rows, width), F32),
        ),
        in_specs=[in_hbm] * 13,
        out_specs=(vmem, vmem),
        scratch_shapes=[
            pltpu.VMEM((rows, model), BF16),
            pltpu.VMEM((model,), F32),
            pltpu.VMEM((model,), F32),
            pltpu.SMEM((requests,), jnp.int32),
            pltpu.SMEM((requests,), jnp.int32),
            pltpu.SMEM((requests,), jnp.int32),
            pltpu.SMEM((1, blocks), jnp.int32),
            pltpu.SMEM((1, blocks), jnp.int32),
            pltpu.VMEM((heads * HD, model), BF16),
            pltpu.VMEM((width, model), BF16),
            pltpu.VMEM((heads * HD, model), BF16),
            pltpu.VMEM((hidden_units, model), BF16),
            pltpu.VMEM((hidden_units, model), BF16),
            pltpu.VMEM((blocks, tokens, width), BF16),
            pltpu.VMEM((kvs, rows, width), BF16),
            pltpu.VMEM((requests, width), F32),
            pltpu.VMEM((kvs, rows, 128), F32),
            pltpu.VMEM((kvs, rows, heads * HD), BF16),
            pltpu.VMEM((sources, rows, 128), F32),
            pltpu.VMEM((sources, rows, heads * HD), BF16),
            pltpu.VMEM((tps, rows, model), BF16),
            pltpu.VMEM((tps, rows, model), BF16),
            dma((8,)),
            dma((2 * heads + 3,)),
            dma((blocks,)),
            dma((kvs,)),
            dma((kvs,)),
            dma((sources,)),
            dma((sources,)),
            dma((sources,)),
            dma((sources,)),
            dma((tps,)),
            dma((tps,)),
            dma((tps,)),
            dma((tps,)),
        ],
        compiler_params=pltpu.CompilerParams(
            collective_id=0, has_side_effects=True, vmem_limit_bytes=56 * 1024 * 1024
        ),
        name="decode_layer",
    )(
        token_state,
        attn_gain,
        mlp_gain,
        home_replica,
        moving,
        cache_length,
        block_owner,
        block_index,
        qkv_weight.T,
        out_weight,
        up_weight.T,
        down_weight,
        kv_cache,
    )


def solution(mesh):
    return jax.shard_map(
        functools.partial(body, mesh.shape["rep"], mesh.shape["kv"], mesh.shape["tp"]),
        mesh=mesh,
        in_specs=(
            P("kv", None),
            P(),
            P(None, "tp"),
            P("tp", None),
            P(),
            P(None, "tp"),
            P("tp", None),
            P("rep", "kv", None, "tp"),
            P(),
            P(),
            P(),
            P("rep", "kv"),
            P("rep", "kv"),
        ),
        out_specs=(P("rep", "kv", None), P("rep", "kv", "tp")),
        check_vma=False,
    )
```
